128 devices in a mesh: pipe: 32 (over z, y, x_hi), head: 4 (over x_lo, core).
Axes of the slice: x: 4 (x_hi: 2, x_lo: 2; x = x_hi * 2 + x_lo), y: 4, z: 4, core: 2. Of those that a mesh axis runs over, the one named last changes fastest.
Arguments:
- queries: bfloat16 [2, 8192, 8192], P(None, 'pipe', 'head'), may hold values from -150 to 150
- keys: bfloat16 [8192, 1024], P(('pipe', 'head')), may hold values from -7 to 7
- values: bfloat16 [8192, 1024], P(('pipe', 'head')), may hold values from -6 to 6
- slice_index: int32 [2, 32], replicated, may hold values from 0 to 31, each once within a row
Outputs:
- attended: bfloat16 [2, 8192, 8192], P(None, 'pipe', 'head')
The draws below stay inside these ranges and needn't reach their ends.
Inputs may be any that keep to these rules, and one draw needn't show every extreme that they name: Each row of slice_index is a permutation of 0 to 31.
All inputs are finite; a program needn't handle non-finite values.
Results may differ from the reference program's by a relative error of at most 0.0041.
Values may be sent and summed in bfloat16 or wider, within the bound.
No kernel may reach another device: no remote copies, remote signals or barrier semaphores. Data moves between devices by JAX's collectives and lax.ppermute only.
A program may use at most 128 MiB of HBM per device.

```python
import jax
import jax.numpy as jnp
from jax import lax

QUERY_HEADS = 64
KEY_VALUE_HEADS = 8
HEAD_SIZE = 128
SLICE_ROWS = 256
TICK_COUNT = 2
SEQUENCE_TOKENS = 8192
N_PIPE = 32


def key_region(key):
    query_field = jax.random.truncated_normal(jax.random.fold_in(key, 11), -6.0, 6.0, (SEQUENCE_TOKENS, KEY_VALUE_HEADS * HEAD_SIZE), jnp.float32)
    return query_field


def draw_keys(key, part):
    return key_region(key).astype(jnp.bfloat16)


def draw_queries(key, part):
    query_field = jax.random.truncated_normal(jax.random.fold_in(key, 21), -6.0, 6.0, (TICK_COUNT, SEQUENCE_TOKENS, QUERY_HEADS * HEAD_SIZE), jnp.float32)
    return query_field.astype(jnp.bfloat16)


def levels(rng, shape, split, least, largest):
    loudness, own = 1.0, jax.random.fold_in(rng, 6)
    for axis_at, shards_of in split:
        draws = jnp.exp(jax.random.uniform(jax.random.fold_in(own, axis_at), (shards_of,), jnp.float32, least / len(split), largest / len(split)))
        loudness = loudness * jnp.repeat(draws, shape[axis_at] // shards_of).reshape([-1 if axis == axis_at else 1 for axis in range(len(shape))])
    return loudness


def centred(own_key, shape, width, reach, shards=(), kind=jnp.bfloat16):
    result = width * jax.random.normal(own_key, shape, jnp.float32)
    if shards:
        result = result * levels(own_key, shape, shards, -0.22, 0.18)
    return jnp.clip(result, -reach, reach).astype(kind)


def setup_inputs(seed: int = 0) -> dict:
    seeds = jax.random.split(jax.random.key(seed), 5)
    return {
        "queries": draw_queries(jax.random.fold_in(seeds[4], 71), 0),
        "keys": draw_keys(jax.random.fold_in(seeds[4], 71), 0),
        "values": centred(seeds[2], (SEQUENCE_TOKENS, KEY_VALUE_HEADS * HEAD_SIZE), 1.0, 6.0, ((0, 128),)),
        "slice_index": jax.vmap(lambda own: jax.random.permutation(own, N_PIPE))(jax.random.split(seeds[3], TICK_COUNT)).reshape((TICK_COUNT, N_PIPE)).astype(jnp.int32),
    }


NEG = -1.0e30


def reference(queries, keys, values, slice_index):
    query_group = QUERY_HEADS // KEY_VALUE_HEADS
    query_matrix = queries.reshape(TICK_COUNT, N_PIPE, SLICE_ROWS, KEY_VALUE_HEADS, query_group, HEAD_SIZE)
    key_matrix = keys.reshape(SEQUENCE_TOKENS, KEY_VALUE_HEADS, HEAD_SIZE)
    value_matrix = values.reshape(SEQUENCE_TOKENS, KEY_VALUE_HEADS, HEAD_SIZE)
    key_pos = jnp.arange(SEQUENCE_TOKENS, dtype=jnp.int32)

    def single_output(item_index):
        tick_index = item_index // (N_PIPE * KEY_VALUE_HEADS)
        section_index = (item_index // KEY_VALUE_HEADS) % N_PIPE
        head_index = item_index % KEY_VALUE_HEADS
        query = query_matrix[tick_index, section_index, :, head_index].astype(jnp.float32)
        key_head = key_matrix[:, head_index].astype(jnp.float32)
        value_head = value_matrix[:, head_index].astype(jnp.float32)
        query_pos = slice_index[tick_index, section_index].astype(jnp.int32) * SLICE_ROWS + jnp.arange(SLICE_ROWS, dtype=jnp.int32)
        scores = jnp.einsum("rgd,kd->rgk", query, key_head) * (HEAD_SIZE ** -0.5)
        allowed = (key_pos[None, :] <= query_pos[:, None])[:, None, :]
        peak = jnp.max(jnp.where(allowed, scores, NEG), axis=-1)
        weights = jnp.where(allowed, jnp.exp(scores - peak[..., None]), 0.0)
        total = jnp.sum(weights, axis=-1)
        numer = jnp.einsum("rgk,kd->rgd", weights.astype(jnp.bfloat16).astype(jnp.float32), value_head)
        return (numer / total[..., None]).astype(jnp.bfloat16)

    output_list = lax.map(single_output, jnp.arange(TICK_COUNT * N_PIPE * KEY_VALUE_HEADS, dtype=jnp.int32))
    output_list = output_list.reshape(TICK_COUNT, N_PIPE, KEY_VALUE_HEADS, SLICE_ROWS, query_group, HEAD_SIZE).transpose(0, 1, 3, 2, 4, 5)
    return output_list.reshape(TICK_COUNT, SEQUENCE_TOKENS, QUERY_HEADS * HEAD_SIZE)
```

```python
import functools
import math

import jax
import jax.numpy as jnp
from jax import lax
from jax.experimental import pallas as pl
from jax.experimental.pallas import tpu as pltpu
from jax.sharding import PartitionSpec as P

HEAD_SIZE = 128
SCALE = HEAD_SIZE ** -0.5 * math.log2(math.e)
NEG = -1e30
UNIT = 512
PIECE = 64
GROUP = UNIT // PIECE
VALUE_ROWS = 144
STATE_ROWS = VALUE_ROWS + 8
LARGE = 2.0**64
VMEM_LIMIT = 36 * 2**20


def pack_body(key_ref, value_ref, *outs):
    head = lax.axis_index("head")
    for at, out in enumerate(outs):
        for half in range(2):
            column = ((head ^ at) * 2 + half) * HEAD_SIZE
            lanes = pl.ds(pl.multiple_of(column, HEAD_SIZE), HEAD_SIZE)
            out[half, 0] = key_ref[:, lanes]
            out[half, 1] = value_ref[:, lanes]


def pack(keys, values):
    heads = keys.shape[1] // HEAD_SIZE
    shape = (2, 2, keys.shape[0], HEAD_SIZE)
    return pl.pallas_call(
        pack_body,
        in_specs=[pl.BlockSpec(memory_space=pltpu.VMEM)] * 2,
        out_specs=[pl.BlockSpec(memory_space=pltpu.VMEM)] * (heads // 2),
        out_shape=[jax.ShapeDtypeStruct(shape, keys.dtype)] * (heads // 2),
        name="pack",
    )(keys, values)


def prepare_body(query_ref, out_ref, *, length):
    for g in range(query_ref.shape[2] // HEAD_SIZE):
        query = query_ref[0, :, g * HEAD_SIZE : (g + 1) * HEAD_SIZE]
        scaled = query.astype(jnp.float32).T * SCALE
        high = scaled.astype(jnp.bfloat16)
        low = (scaled - high.astype(jnp.float32)).astype(jnp.bfloat16)
        out_ref[:HEAD_SIZE, g * length : (g + 1) * length] = high
        out_ref[HEAD_SIZE:, g * length : (g + 1) * length] = low


def prepare(queries):
    ticks, length, columns = queries.shape
    rows = columns // 2 // HEAD_SIZE * length
    return pl.pallas_call(
        functools.partial(prepare_body, length=length),
        grid=(ticks, 2),
        in_specs=[pl.BlockSpec((1, length, columns // 2), lambda t, h: (t, 0, h))],
        out_specs=pl.BlockSpec(
            (None, None, 2 * HEAD_SIZE, rows), lambda t, h: (t, h, 0, 0)
        ),
        out_shape=jax.ShapeDtypeStruct(
            (ticks, 2, 2 * HEAD_SIZE, rows), jnp.bfloat16
        ),
        compiler_params=pltpu.CompilerParams(vmem_limit_bytes=VMEM_LIMIT),
        name="prepare",
        cost_estimate=pl.CostEstimate(flops=0, bytes_accessed=6 * 2**20, transcendentals=0),
    )(queries)


def attend_body(slices, *refs, units, places, length, first, last):
    refs = list(refs)
    query_ref = refs.pop(0)
    blocks = [[refs.pop(0) for _ in units[0]], [refs.pop(0) for _ in units[1]]]
    before = None if first else refs.pop(0)
    out_ref = refs.pop(0)
    state, key_buf, value_buf = refs if last else [out_ref] + refs
    count = sum(units[0])
    half, tick = pl.program_id(0), pl.program_id(1)
    rows = query_ref.shape[1]
    pipe = lax.axis_index("pipe")
    mine = (pipe & 1) * 4 + lax.axis_index("head")
    ids = [
        [
            (((pipe >> 3) + dz) & 3) * 4 + (((pipe >> 1) + dy) & 3)
            for dz, dy in listed
        ]
        for listed in places
    ]

    for which in range(2):

        @pl.when((half == which) & (tick == 0))
        def _(which=which):
            at = 0
            for block, many in zip(blocks[which], units[which]):
                for j in range(many):
                    slot = sum(
                        jnp.where(other < ids[which][at], 1, 0) for other in ids[which]
                    )
                    key_buf[slot] = block[j, :, 0].reshape(UNIT, HEAD_SIZE)
                    value_buf[slot, :HEAD_SIZE] = block[j, :, 1].reshape(UNIT, HEAD_SIZE).T
                    value_buf[slot, HEAD_SIZE:] = jnp.ones(
                        (VALUE_ROWS - HEAD_SIZE, UNIT), jnp.bfloat16
                    )
                    at += 1

    where = slices[tick, pipe]
    seen, final = jnp.int32(0), jnp.int32(0)
    for at in range(count):
        unit = jnp.where(half == 0, ids[0][at], ids[1][at])
        visible = unit * UNIT <= where * length
        seen += jnp.where(visible, 1, 0)
        final = jnp.maximum(final, jnp.where(visible, unit, 0))
    lead = where * length - final * UNIT

    def scores(keys):
        return jnp.dot(
            jnp.concatenate([keys, keys], axis=1),
            query_ref[...],
            preferred_element_type=jnp.float32,
        )

    def exact(i, carry):
        slot = seen - 1 - i
        value = scores(key_buf[slot])
        key_at = lax.broadcasted_iota(jnp.int32, (UNIT, rows), 0)
        key_at = (((key_at >> 6) ^ mine) << 6) + (key_at & (PIECE - 1))
        query_at = lax.broadcasted_iota(jnp.int32, (UNIT, rows), 1) & (length - 1)
        reach = jnp.where(i == 0, lead, UNIT)
        value = jnp.where(key_at - query_at <= reach, value, NEG)
        old = state[VALUE_ROWS : VALUE_ROWS + 1, :]
        peak = jnp.maximum(old, jnp.max(value, axis=0, keepdims=True))
        weights = jnp.exp2(value - peak).astype(jnp.bfloat16)
        part = jnp.dot(value_buf[slot], weights, preferred_element_type=jnp.float32)
        state[:VALUE_ROWS] = state[:VALUE_ROWS] * jnp.exp2(old - peak) + part
        state[VALUE_ROWS:] = jnp.broadcast_to(peak, (8, rows))
        return carry

    def rest(slot, many):
        keys = key_buf[pl.ds(slot, many)].reshape(many * UNIT, HEAD_SIZE)
        weights = jnp.exp2(scores(keys) - state[VALUE_ROWS : VALUE_ROWS + 1, :])
        values = [value_buf[slot + j] for j in range(many)]
        values = values[0] if many == 1 else jnp.concatenate(values, axis=1)
        state[:VALUE_ROWS] += jnp.dot(
            values, weights.astype(jnp.bfloat16), preferred_element_type=jnp.float32
        )

    def attempt(carry):
        tried, _ = carry
        if first:
            state[:VALUE_ROWS] = jnp.zeros((VALUE_ROWS, rows), jnp.float32)
            state[VALUE_ROWS:] = jnp.full((8, rows), NEG, jnp.float32)
        else:
            state[...] = before[...]
        careful = jnp.where(tried == 0, jnp.minimum(seen, 1), seen)
        lax.fori_loop(0, careful, exact, 0)
        left = seen - careful

        def pair(i, c):
            rest(i * 2, 2)
            return c

        lax.fori_loop(0, left // 2, pair, 0)

        @pl.when(left % 2 == 1)
        def _():
            rest(left - 1, 1)

        worst = jnp.max(state[HEAD_SIZE : HEAD_SIZE + 1, :])
        fine = worst < LARGE
        return tried + 1, jnp.where(fine, 0, 1)

    lax.while_loop(
        lambda carry: (carry[0] == 0) | ((carry[0] == 1) & (carry[1] == 1)),
        attempt,
        (jnp.int32(0), jnp.int32(0)),
    )

    if last:
        for g in range(rows // length):
            columns = slice(g * length, (g + 1) * length)
            total = state[HEAD_SIZE : HEAD_SIZE + 1, columns]
            result = (state[:HEAD_SIZE, columns] / total).T
            out_ref[0, :, g * HEAD_SIZE : (g + 1) * HEAD_SIZE] = result.astype(
                jnp.bfloat16
            )


def attend(slices, query, blocks, places, before, length, last):
    ticks, _, depth, rows = query.shape
    units = tuple(tuple(b.shape[0] for b in half) for half in blocks)
    count = sum(units[0])
    flat = [*blocks[0], *blocks[1]]
    first = before is None
    state_spec = pl.BlockSpec((None, None, STATE_ROWS, rows), lambda h, t: (t, h, 0, 0))
    state_shape = (ticks, 2, STATE_ROWS, rows)
    in_specs = [
        pl.BlockSpec(memory_space=pltpu.SMEM),
        pl.BlockSpec((None, None, depth, rows), lambda h, t: (t, h, 0, 0)),
    ]
    in_specs += [pl.BlockSpec(memory_space=pltpu.VMEM)] * len(flat)
    args = [slices, query, *flat]
    if not first:
        in_specs.append(state_spec)
        args.append(before)
    scratch = [
        pltpu.VMEM((count, UNIT, HEAD_SIZE), jnp.bfloat16),
        pltpu.VMEM((count, VALUE_ROWS, UNIT), jnp.bfloat16),
    ]
    if last:
        group = rows // length
        out_specs = pl.BlockSpec((1, length, group * HEAD_SIZE), lambda h, t: (t, 0, h))
        out_shape = jax.ShapeDtypeStruct(
            (ticks, length, 2 * group * HEAD_SIZE), jnp.bfloat16
        )
        scratch = [pltpu.VMEM((STATE_ROWS, rows), jnp.float32)] + scratch
    else:
        out_specs = state_spec
        out_shape = jax.ShapeDtypeStruct(state_shape, jnp.float32)
    return pl.pallas_call(
        functools.partial(
            attend_body,
            units=units,
            places=places,
            length=length,
            first=first,
            last=last,
        ),
        grid=(2, ticks),
        in_specs=in_specs,
        out_specs=out_specs,
        out_shape=out_shape,
        scratch_shapes=scratch,
        compiler_params=pltpu.CompilerParams(vmem_limit_bytes=VMEM_LIMIT),
        cost_estimate=pl.CostEstimate(
            flops=2 * ticks * count * UNIT * rows * 2 * HEAD_SIZE * 2,
            bytes_accessed=16 * 2**20,
            transcendentals=2 * ticks * count * UNIT * rows,
        ),
        name=f"attend_{count}",
    )(*args)


def on_device(queries, keys, values, slice_index):
    length = queries.shape[1]
    axes = ("pipe", "head")
    pieces = pack(keys, values)
    got = [pieces[0]]
    for j in range(1, GROUP):
        swap = [(i, i ^ j) for i in range(32 * 4)]
        got.append(lax.ppermute(pieces[j & 3], axes, swap))
    query = prepare(queries)
    both = jnp.stack(got, axis=1)

    def shift(x, dim, step):
        stride = 8 if dim == "z" else 2
        table = []
        for i in range(32):
            at = (i // stride) % 4
            table.append((i, i + ((at + step) % 4 - at) * stride))
        return lax.ppermute(x, "pipe", table)

    stages = []
    for half, (near, far) in enumerate((("y", "z"), ("z", "y"))):
        unit = both[half]
        right = shift(unit, near, 1)
        left = shift(unit, near, -1)
        c1 = jnp.stack([unit, right])
        r1 = shift(c1, far, 1)
        l1 = shift(c1, far, -1)
        middle = GROUP // 2
        opposite = jnp.concatenate(
            [shift(right[:middle], near, 1), shift(left[middle:], near, -1)]
        )
        c2 = jnp.stack([left, opposite])
        r2 = shift(c2, far, 1)
        l2 = shift(c2, far, -1)
        stages.append(([c1, c2], [r1, l1, r2, l2]))

    c1, c2 = [(0, 0), (0, -1)], [(0, 1), (0, 2)]
    places = (
        c1 + c2,
        [(f, n) for part in (c1, c2) for f in (-1, 1) for _, n in part],
        [(2, n) for _, n in c1 + c2],
    )
    places = [([(f, n) for f, n in p], [(n, f) for f, n in p]) for p in places]

    def run(at, blocks, before):
        return attend(slice_index, query, blocks, places[at], before, length, at == 2)

    state = run(0, [stage[0] for stage in stages], None)
    near, state = lax.optimization_barrier(([stage[1] for stage in stages], state))
    opposite = [
        [shift(r1, far, 1), shift(l2, far, -1)]
        for (r1, l1, r2, l2), far in zip(near, ("z", "y"))
    ]
    state = run(1, near, state)
    return run(2, opposite, state)


def solution(mesh):
    return jax.shard_map(
        on_device,
        mesh=mesh,
        in_specs=(
            P(None, "pipe", "head"),
            P(("pipe", "head"), None),
            P(("pipe", "head"), None),
            P(),
        ),
        out_specs=P(None, "pipe", "head"),
        check_vma=False,
    )
```

```python
import functools
import math

import jax
import jax.numpy as jnp
from jax import lax
from jax.experimental import pallas as pl
from jax.experimental.pallas import tpu as pltpu
from jax.sharding import PartitionSpec as P

HEAD_SIZE = 128
SCALE = HEAD_SIZE ** -0.5 * math.log2(math.e)
NEG = -1e30
UNIT = 512
PIECE = 64
GROUP = UNIT // PIECE
VALUE_ROWS = 144
STATE_ROWS = VALUE_ROWS + 8
LARGE = 2.0**100
VMEM_LIMIT = 36 * 2**20


def pack_body(key_ref, value_ref, out_ref):
    for head in range(4):
        for half in range(2):
            column = (head * 2 + half) * HEAD_SIZE
            lanes = slice(column, column + HEAD_SIZE)
            for to in (head, head + 4):
                out_ref[to, half, 0] = key_ref[:, lanes]
                out_ref[to, half, 1] = value_ref[:, lanes]


def pack(keys, values):
    return pl.pallas_call(
        pack_body,
        in_specs=[pl.BlockSpec(memory_space=pltpu.VMEM)] * 2,
        out_specs=pl.BlockSpec(memory_space=pltpu.VMEM),
        out_shape=jax.ShapeDtypeStruct(
            (GROUP, 2, 2, keys.shape[0], HEAD_SIZE), keys.dtype
        ),
        name="pack",
    )(keys, values)


def prepare_body(query_ref, out_ref, *, length):
    for g in range(query_ref.shape[2] // HEAD_SIZE):
        query = query_ref[0, :, g * HEAD_SIZE : (g + 1) * HEAD_SIZE]
        scaled = query.astype(jnp.float32).T * SCALE
        high = scaled.astype(jnp.bfloat16)
        low = (scaled - high.astype(jnp.float32)).astype(jnp.bfloat16)
        out_ref[:HEAD_SIZE, g * length : (g + 1) * length] = high
        out_ref[HEAD_SIZE:, g * length : (g + 1) * length] = low


def prepare(queries):
    ticks, length, columns = queries.shape
    rows = columns // 2 // HEAD_SIZE * length
    return pl.pallas_call(
        functools.partial(prepare_body, length=length),
        grid=(ticks, 2),
        in_specs=[pl.BlockSpec((1, length, columns // 2), lambda t, h: (t, 0, h))],
        out_specs=pl.BlockSpec(
            (None, None, 2 * HEAD_SIZE, rows), lambda t, h: (t, h, 0, 0)
        ),
        out_shape=jax.ShapeDtypeStruct(
            (ticks, 2, 2 * HEAD_SIZE, rows), jnp.bfloat16
        ),
        compiler_params=pltpu.CompilerParams(vmem_limit_bytes=VMEM_LIMIT),
        name="prepare",
        cost_estimate=pl.CostEstimate(flops=0, bytes_accessed=6 * 2**20, transcendentals=0),
    )(queries)


def attend_body(slices, *refs, units, places, earlier, length, first, last):
    refs = list(refs)
    query_ref = refs.pop(0)
    blocks = [[refs.pop(0) for _ in units[0]], [refs.pop(0) for _ in units[1]]]
    before = None if first else refs.pop(0)
    out_ref = refs.pop(0)
    state, key_buf, value_buf = refs if last else [out_ref] + refs
    count = sum(units[0])
    half, tick = pl.program_id(0), pl.program_id(1)
    rows = query_ref.shape[1]
    pipe = lax.axis_index("pipe")

    def numbered(listed):
        return [
            (((pipe >> 3) + dz) & 3) * 4 + (((pipe >> 1) + dy) & 3)
            for dz, dy in listed
        ]

    ids = [numbered(listed) for listed in places]

    for which in range(2):

        @pl.when((half == which) & (tick == 0))
        def _(which=which):
            at = 0
            for block, many in zip(blocks[which], units[which]):
                for j in range(many):
                    slot = sum(
                        jnp.where(other < ids[which][at], 1, 0) for other in ids[which]
                    )
                    key_buf[slot] = block[j, :, 0].reshape(UNIT, HEAD_SIZE)
                    value_buf[slot, :HEAD_SIZE] = block[j, :, 1].reshape(UNIT, HEAD_SIZE).T
                    value_buf[slot, HEAD_SIZE:] = jnp.ones(
                        (VALUE_ROWS - HEAD_SIZE, UNIT), jnp.bfloat16
                    )
                    at += 1

    where = slices[tick, pipe]
    seen, final = jnp.int32(0), jnp.int32(0)
    for one, other in zip(*ids):
        unit = jnp.where(half == 0, one, other)
        visible = unit * UNIT <= where * length
        seen += jnp.where(visible, 1, 0)
        final = jnp.maximum(final, jnp.where(visible, unit, 0))
    lead = where * length - final * UNIT
    blank = seen > 0
    for one, other in zip(*[numbered(listed) for listed in earlier]):
        blank &= jnp.where(half == 0, one, other) * UNIT > where * length

    def scores(keys):
        return jnp.dot(
            jnp.concatenate([keys, keys], axis=1),
            query_ref[...],
            preferred_element_type=jnp.float32,
        )

    def mask(value, reach):
        key_at = lax.broadcasted_iota(jnp.int32, value.shape, 0)
        query_at = lax.broadcasted_iota(jnp.int32, value.shape, 1) & (length - 1)
        return jnp.where(key_at - query_at <= reach, value, NEG)

    def values_of(slot, many):
        values = [value_buf[slot + j] for j in range(many)]
        return values[0] if many == 1 else jnp.concatenate(values, axis=1)

    def with_peak():
        value = mask(scores(key_buf[seen - 1, :16]), lead)
        peak = jnp.max(value, axis=0, keepdims=True)
        state[VALUE_ROWS:] = jnp.broadcast_to(peak, (8, rows))

    def add(slot, many, reach=None):
        keys = key_buf[pl.ds(slot, many)].reshape(many * UNIT, HEAD_SIZE)
        value = scores(keys)
        if reach is not None:
            value = mask(value, reach)
        weights = jnp.exp2(value - state[VALUE_ROWS : VALUE_ROWS + 1, :])
        state[:VALUE_ROWS] += jnp.dot(
            values_of(slot, many),
            weights.astype(jnp.bfloat16),
            preferred_element_type=jnp.float32,
        )

    def exact(slot, carry):
        reach = jnp.where(slot == seen - 1, lead, UNIT)
        value = mask(scores(key_buf[slot]), reach)
        old = state[VALUE_ROWS : VALUE_ROWS + 1, :]
        peak = jnp.maximum(old, jnp.max(value, axis=0, keepdims=True))
        weights = jnp.exp2(value - peak).astype(jnp.bfloat16)
        part = jnp.dot(value_buf[slot], weights, preferred_element_type=jnp.float32)
        state[:VALUE_ROWS] = state[:VALUE_ROWS] * jnp.exp2(old - peak) + part
        state[VALUE_ROWS:] = jnp.broadcast_to(peak, (8, rows))
        return carry

    def start():
        if first:
            state[:VALUE_ROWS] = jnp.zeros((VALUE_ROWS, rows), jnp.float32)
            state[VALUE_ROWS:] = jnp.full((8, rows), NEG, jnp.float32)
        else:
            state[...] = before[...]

    start()
    pl.when(blank)(with_peak)
    whole = jnp.where(lead < UNIT, jnp.maximum(seen - 1, 0), seen)

    def pair(i, carry):
        add(i * 2, 2)
        return carry

    lax.fori_loop(0, whole >> 1, pair, 0)
    tail = seen - (whole >> 1) * 2

    @pl.when(tail == 1)
    def _():
        add(seen - 1, 1, lead)

    if count > 1:

        @pl.when(tail == 2)
        def _():
            add(seen - 2, 2, lead + UNIT)

    @pl.when(jnp.logical_not(jnp.max(state[HEAD_SIZE : HEAD_SIZE + 1, :]) < LARGE))
    def _():
        start()
        lax.fori_loop(0, seen, exact, 0)

    if last:
        for g in range(rows // length):
            columns = slice(g * length, (g + 1) * length)
            total = state[HEAD_SIZE : HEAD_SIZE + 1, columns]
            result = (state[:HEAD_SIZE, columns] / total).T
            out_ref[0, :, g * HEAD_SIZE : (g + 1) * HEAD_SIZE] = result.astype(
                jnp.bfloat16
            )


def attend(slices, query, blocks, places, earlier, before, length, last):
    ticks, _, depth, rows = query.shape
    units = tuple(tuple(b.shape[0] for b in half) for half in blocks)
    count = sum(units[0])
    flat = [*blocks[0], *blocks[1]]
    first = before is None
    state_spec = pl.BlockSpec((None, None, STATE_ROWS, rows), lambda h, t: (t, h, 0, 0))
    state_shape = (ticks, 2, STATE_ROWS, rows)
    in_specs = [
        pl.BlockSpec(memory_space=pltpu.SMEM),
        pl.BlockSpec((None, None, depth, rows), lambda h, t: (t, h, 0, 0)),
    ]
    in_specs += [pl.BlockSpec(memory_space=pltpu.VMEM)] * len(flat)
    args = [slices, query, *flat]
    if not first:
        in_specs.append(state_spec)
        args.append(before)
    scratch = [
        pltpu.VMEM((count, UNIT, HEAD_SIZE), jnp.bfloat16),
        pltpu.VMEM((count, VALUE_ROWS, UNIT), jnp.bfloat16),
    ]
    if last:
        group = rows // length
        out_specs = pl.BlockSpec((1, length, group * HEAD_SIZE), lambda h, t: (t, 0, h))
        out_shape = jax.ShapeDtypeStruct(
            (ticks, length, 2 * group * HEAD_SIZE), jnp.bfloat16
        )
        scratch = [pltpu.VMEM((STATE_ROWS, rows), jnp.float32)] + scratch
    else:
        out_specs = state_spec
        out_shape = jax.ShapeDtypeStruct(state_shape, jnp.float32)
    return pl.pallas_call(
        functools.partial(
            attend_body,
            units=units,
            places=places,
            earlier=earlier,
            length=length,
            first=first,
            last=last,
        ),
        grid=(2, ticks),
        in_specs=in_specs,
        out_specs=out_specs,
        out_shape=out_shape,
        scratch_shapes=scratch,
        compiler_params=pltpu.CompilerParams(vmem_limit_bytes=VMEM_LIMIT),
        cost_estimate=pl.CostEstimate(
            flops=2 * ticks * count * UNIT * rows * 2 * HEAD_SIZE * 2,
            bytes_accessed=16 * 2**20,
            transcendentals=2 * ticks * count * UNIT * rows,
        ),
        name=f"attend_{count}",
    )(*args)


def on_device(queries, keys, values, slice_index):
    length = queries.shape[1]
    groups = [list(range(i, i + GROUP)) for i in range(0, 32 * 4, GROUP)]
    both = lax.all_to_all(
        pack(keys, values),
        ("pipe", "head"),
        split_axis=0,
        concat_axis=0,
        axis_index_groups=groups,
        tiled=True,
    )
    query = prepare(queries)

    def shift(x, dim, step):
        stride = 8 if dim == "z" else 2
        table = []
        for i in range(32):
            at = (i // stride) % 4
            table.append((i, i + ((at + step) % 4 - at) * stride))
        return lax.ppermute(x, "pipe", table)

    stages = []
    for half, (near, far) in enumerate((("y", "z"), ("z", "y"))):
        unit = both[:, half]
        right = shift(unit, near, 1)
        left = shift(unit, near, -1)
        c1 = jnp.stack([unit, right])
        r1 = shift(c1, far, 1)
        l1 = shift(c1, far, -1)
        middle = GROUP // 2
        opposite = jnp.concatenate(
            [shift(right[:middle], near, 1), shift(left[middle:], near, -1)]
        )
        c2 = jnp.stack([left, opposite])
        r2 = shift(c2, far, 1)
        l2 = shift(c2, far, -1)
        stages.append(([c1, c2], [r1, l1, r2, l2]))

    c1, c2 = [(0, 0), (0, -1)], [(0, 1), (0, 2)]
    places = (
        c1 + c2,
        [(f, n) for part in (c1, c2) for f in (-1, 1) for _, n in part],
        [(2, n) for _, n in c1 + c2],
    )
    places = [([(f, n) for f, n in p], [(n, f) for f, n in p]) for p in places]

    def run(at, blocks, before):
        earlier = [sum((p[half] for p in places[:at]), []) for half in range(2)]
        return attend(
            slice_index, query, blocks, places[at], earlier, before, length, at == 2
        )

    state = run(0, [stage[0] for stage in stages], None)
    near, state = lax.optimization_barrier(([stage[1] for stage in stages], state))
    opposite = [
        [shift(r1, far, 1), shift(l2, far, -1)]
        for (r1, l1, r2, l2), far in zip(near, ("z", "y"))
    ]
    state = run(1, near, state)
    return run(2, opposite, state)


def solution(mesh):
    return jax.shard_map(
        on_device,
        mesh=mesh,
        in_specs=(
            P(None, "pipe", "head"),
            P(("pipe", "head"), None),
            P(("pipe", "head"), None),
            P(),
        ),
        out_specs=P(None, "pipe", "head"),
        check_vma=False,
    )
```

```python
import functools
import math

import jax
import jax.numpy as jnp
from jax import lax
from jax.experimental import pallas as pl
from jax.experimental.pallas import tpu as pltpu
from jax.sharding import PartitionSpec as P

HEAD_SIZE = 128
SCALE = HEAD_SIZE ** -0.5 * math.log2(math.e)
NEG = -1e30
UNIT = 512
PIECE = 64
GROUP = UNIT // PIECE
PEAK_ROW = HEAD_SIZE + 8
STATE_ROWS = PEAK_ROW + 8
WIDE = 4
LARGE = 2.0**100
COLUMNS = 512
VMEM_LIMIT = 36 * 2**20


def pack_body(key_ref, value_ref, out_ref):
    for head in range(4):
        for half in range(2):
            column = (head * 2 + half) * HEAD_SIZE
            lanes = slice(column, column + HEAD_SIZE)
            for to in (head, head + 4):
                out_ref[to, half, 0] = key_ref[:, lanes]
                out_ref[to, half, 1] = value_ref[:, lanes]


def pack(keys, values):
    return pl.pallas_call(
        pack_body,
        in_specs=[pl.BlockSpec(memory_space=pltpu.VMEM)] * 2,
        out_specs=pl.BlockSpec(memory_space=pltpu.VMEM),
        out_shape=jax.ShapeDtypeStruct(
            (GROUP, 2, 2, keys.shape[0], HEAD_SIZE), keys.dtype
        ),
        name="pack",
    )(keys, values)


def prepare_body(query_ref, out_ref, *, length):
    for g in range(query_ref.shape[2] // HEAD_SIZE):
        query = query_ref[0, :, g * HEAD_SIZE : (g + 1) * HEAD_SIZE]
        scaled = query.astype(jnp.float32).T * SCALE
        high = scaled.astype(jnp.bfloat16)
        low = (scaled - high.astype(jnp.float32)).astype(jnp.bfloat16)
        out_ref[:HEAD_SIZE, g * length : (g + 1) * length] = high
        out_ref[HEAD_SIZE:, g * length : (g + 1) * length] = low


def prepare(queries):
    ticks, length, columns = queries.shape
    rows = columns // 2 // HEAD_SIZE * length
    return pl.pallas_call(
        functools.partial(prepare_body, length=length),
        grid=(ticks, 2),
        in_specs=[pl.BlockSpec((1, length, columns // 2), lambda t, h: (t, 0, h))],
        out_specs=pl.BlockSpec(
            (None, None, 2 * HEAD_SIZE, rows), lambda t, h: (t, h, 0, 0)
        ),
        out_shape=jax.ShapeDtypeStruct(
            (ticks, 2, 2 * HEAD_SIZE, rows), jnp.bfloat16
        ),
        compiler_params=pltpu.CompilerParams(vmem_limit_bytes=VMEM_LIMIT),
        name="prepare",
        cost_estimate=pl.CostEstimate(flops=0, bytes_accessed=6 * 2**20, transcendentals=0),
    )(queries)


def attend_body(slices, *refs, units, places, earlier, length, first, last):
    refs = list(refs)
    query_ref = refs.pop(0)
    blocks = [[refs.pop(0) for _ in units[0]], [refs.pop(0) for _ in units[1]]]
    before = None if first else refs.pop(0)
    out_ref = refs.pop(0)
    state, key_buf, value_buf = refs if last else [out_ref] + refs
    count = sum(units[0])
    half, tick = pl.program_id(0), pl.program_id(1)
    rows = query_ref.shape[1]
    pipe = lax.axis_index("pipe")

    def numbered(listed):
        return [
            (((pipe >> 3) + dz) & 3) * 4 + (((pipe >> 1) + dy) & 3)
            for dz, dy in listed
        ]

    ids = [numbered(listed) for listed in places]

    def lanes_of(slot):
        return pl.ds(pl.multiple_of((slot & (WIDE - 1)) * UNIT, UNIT), UNIT)

    for which in range(2):

        @pl.when((half == which) & (tick == 0))
        def _(which=which):
            at = 0
            for block, many in zip(blocks[which], units[which]):
                for j in range(many):
                    slot = sum(
                        jnp.where(other < ids[which][at], 1, 0) for other in ids[which]
                    )
                    key_buf[slot] = block[j, :, 0].reshape(UNIT, HEAD_SIZE)
                    value_buf[slot // WIDE, :, lanes_of(slot)] = (
                        block[j, :, 1].reshape(UNIT, HEAD_SIZE).T
                    )
                    at += 1

    where = slices[tick, pipe]
    seen, final = jnp.int32(0), jnp.int32(0)
    for one, other in zip(*ids):
        unit = jnp.where(half == 0, one, other)
        visible = unit * UNIT <= where * length
        seen += jnp.where(visible, 1, 0)
        final = jnp.maximum(final, jnp.where(visible, unit, 0))
    lead = where * length - final * UNIT
    blank = seen > 0
    for one, other in zip(*[numbered(listed) for listed in earlier]):
        blank &= jnp.where(half == 0, one, other) * UNIT > where * length

    def scores(keys):
        return jnp.dot(
            jnp.concatenate([keys, keys], axis=1),
            query_ref[...],
            preferred_element_type=jnp.float32,
        )

    def mask(value, reach):
        key_at = lax.broadcasted_iota(jnp.int32, value.shape, 0)
        query_at = lax.broadcasted_iota(jnp.int32, value.shape, 1) & (length - 1)
        return jnp.where(key_at - query_at <= reach, value, NEG)

    def with_peak():
        value = mask(scores(key_buf[seen - 1, :16]), lead)
        peak = jnp.max(value, axis=0, keepdims=True)
        state[PEAK_ROW:] = jnp.broadcast_to(peak, (8, rows))

    def add(slot, many, reach=None, at=0):
        keys = key_buf[pl.ds(slot, many)].reshape(many * UNIT, HEAD_SIZE)
        keys = jnp.concatenate([keys, keys], axis=1)
        lanes = pl.ds(pl.multiple_of(at * UNIT, UNIT), many * UNIT)
        values = value_buf[slot // WIDE, :, lanes]
        for column in range(0, rows, COLUMNS):
            here = slice(column, column + COLUMNS)
            value = jnp.dot(
                keys, query_ref[:, here], preferred_element_type=jnp.float32
            )
            if reach is not None:
                value = mask(value, reach)
            weights = jnp.exp2(value - state[PEAK_ROW : PEAK_ROW + 1, here])
            state[HEAD_SIZE:PEAK_ROW, here] += jnp.sum(
                weights.reshape(-1, 8, COLUMNS), axis=0
            )
            state[:HEAD_SIZE, here] += jnp.dot(
                values,
                weights.astype(jnp.bfloat16),
                preferred_element_type=jnp.float32,
            )

    def exact(slot, carry):
        reach = jnp.where(slot == seen - 1, lead, UNIT)
        value = mask(scores(key_buf[slot]), reach)
        old = state[PEAK_ROW : PEAK_ROW + 1, :]
        peak = jnp.maximum(old, jnp.max(value, axis=0, keepdims=True))
        weights = jnp.exp2(value - peak)
        part = jnp.dot(
            value_buf[slot // WIDE, :, lanes_of(slot)],
            weights.astype(jnp.bfloat16),
            preferred_element_type=jnp.float32,
        )
        factor = jnp.exp2(old - peak)
        state[:HEAD_SIZE] = state[:HEAD_SIZE] * factor + part
        total = jnp.sum(weights.reshape(-1, 8, rows), axis=0)
        state[HEAD_SIZE:PEAK_ROW] = state[HEAD_SIZE:PEAK_ROW] * factor + total
        state[PEAK_ROW:] = jnp.broadcast_to(peak, (8, rows))
        return carry

    def start():
        if first:
            state[:PEAK_ROW] = jnp.zeros((PEAK_ROW, rows), jnp.float32)
            state[PEAK_ROW:] = jnp.full((8, rows), NEG, jnp.float32)
        else:
            state[...] = before[...]

    start()
    pl.when(blank)(with_peak)
    whole = jnp.where(lead < UNIT, jnp.maximum(seen - 1, 0), seen)

    def wide(i, carry):
        add(i * WIDE, WIDE)
        return carry

    if count >= WIDE:
        lax.fori_loop(0, whole // WIDE, wide, 0)

    if count > 2:

        @pl.when((whole & 2) != 0)
        def _():
            slot = whole // WIDE * WIDE
            add(slot, 2)

    tail = seen - whole // 2 * 2

    @pl.when(tail == 1)
    def _():
        add(seen - 1, 1, lead, (seen - 1) & 2)

    if count > 1:

        @pl.when(tail == 2)
        def _():
            add(seen - 2, 2, lead + UNIT, (seen - 2) & 2)

    @pl.when(jnp.logical_not(jnp.max(state[HEAD_SIZE:PEAK_ROW]) < LARGE))
    def _():
        start()
        lax.fori_loop(0, seen, exact, 0)

    if last:
        for g in range(rows // length):
            columns = slice(g * length, (g + 1) * length)
            total = jnp.sum(state[HEAD_SIZE:PEAK_ROW, columns], axis=0, keepdims=True)
            result = (state[:HEAD_SIZE, columns] / total).T
            out_ref[0, :, g * HEAD_SIZE : (g + 1) * HEAD_SIZE] = result.astype(
                jnp.bfloat16
            )


def attend(slices, query, blocks, places, earlier, before, length, last):
    ticks, _, depth, rows = query.shape
    units = tuple(tuple(b.shape[0] for b in half) for half in blocks)
    count = sum(units[0])
    flat = [*blocks[0], *blocks[1]]
    first = before is None
    state_spec = pl.BlockSpec((None, None, STATE_ROWS, rows), lambda h, t: (t, h, 0, 0))
    state_shape = (ticks, 2, STATE_ROWS, rows)
    in_specs = [
        pl.BlockSpec(memory_space=pltpu.SMEM),
        pl.BlockSpec((None, None, depth, rows), lambda h, t: (t, h, 0, 0)),
    ]
    in_specs += [pl.BlockSpec(memory_space=pltpu.VMEM)] * len(flat)
    args = [slices, query, *flat]
    if not first:
        in_specs.append(state_spec)
        args.append(before)
    scratch = [
        pltpu.VMEM((count, UNIT, HEAD_SIZE), jnp.bfloat16),
        pltpu.VMEM((-(-count // WIDE), HEAD_SIZE, WIDE * UNIT), jnp.bfloat16),
    ]
    if last:
        group = rows // length
        out_specs = pl.BlockSpec((1, length, group * HEAD_SIZE), lambda h, t: (t, 0, h))
        out_shape = jax.ShapeDtypeStruct(
            (ticks, length, 2 * group * HEAD_SIZE), jnp.bfloat16
        )
        scratch = [pltpu.VMEM((STATE_ROWS, rows), jnp.float32)] + scratch
    else:
        out_specs = state_spec
        out_shape = jax.ShapeDtypeStruct(state_shape, jnp.float32)
    return pl.pallas_call(
        functools.partial(
            attend_body,
            units=units,
            places=places,
            earlier=earlier,
            length=length,
            first=first,
            last=last,
        ),
        grid=(2, ticks),
        in_specs=in_specs,
        out_specs=out_specs,
        out_shape=out_shape,
        scratch_shapes=scratch,
        compiler_params=pltpu.CompilerParams(vmem_limit_bytes=VMEM_LIMIT),
        cost_estimate=pl.CostEstimate(
            flops=2 * ticks * count * UNIT * rows * 2 * HEAD_SIZE * 2,
            bytes_accessed=16 * 2**20,
            transcendentals=2 * ticks * count * UNIT * rows,
        ),
        name=f"attend_{count}",
    )(*args)


def on_device(queries, keys, values, slice_index):
    length = queries.shape[1]
    groups = [list(range(i, i + GROUP)) for i in range(0, 32 * 4, GROUP)]
    both = lax.all_to_all(
        pack(keys, values),
        ("pipe", "head"),
        split_axis=0,
        concat_axis=0,
        axis_index_groups=groups,
        tiled=True,
    )
    query = prepare(queries)

    def shift(x, dim, step):
        stride = 8 if dim == "z" else 2
        table = []
        for i in range(32):
            at = (i // stride) % 4
            table.append((i, i + ((at + step) % 4 - at) * stride))
        return lax.ppermute(x, "pipe", table)

    axes = (("y", "z"), ("z", "y"))
    own = [both[:, half] for half in range(2)]
    right = [shift(own[half], axes[half][0], 1) for half in range(2)]
    left = [shift(own[half], axes[half][0], -1) for half in range(2)]
    opposite = [shift(own[half], axes[half][0], 2) for half in range(2)]
    c1 = [jnp.stack([own[half], right[half]]) for half in range(2)]
    r1 = [shift(c1[half], axes[half][1], 1) for half in range(2)]
    l1 = [shift(c1[half], axes[half][1], -1) for half in range(2)]

    p1, p2 = [(0, 0), (0, -1)], [(0, 1), (0, 2)]
    places = (
        p1 + p2[:1],
        p2[1:] + [(f, n) for f in (-1, 1) for _, n in p1],
        [(f, n) for f in (-1, 1) for _, n in p2],
        [(2, n) for _, n in p1 + p2],
    )
    places = [([(f, n) for f, n in p], [(n, f) for f, n in p]) for p in places]

    def run(at, blocks, before):
        earlier = [sum((p[half] for p in places[:at]), []) for half in range(2)]
        return attend(
            slice_index, query, blocks, places[at], earlier, before, length, at == 3
        )

    state = run(0, [(c1[half], left[half][None]) for half in range(2)], None)
    left, opposite, state = lax.optimization_barrier((left, opposite, state))
    c2 = [jnp.stack([left[half], opposite[half]]) for half in range(2)]
    r2 = [shift(c2[half], axes[half][1], 1) for half in range(2)]
    l2 = [shift(c2[half], axes[half][1], -1) for half in range(2)]
    blocks = [(opposite[half][None], r1[half], l1[half]) for half in range(2)]
    state = run(1, blocks, state)
    r1, r2, l2, state = lax.optimization_barrier((r1, r2, l2, state))
    f1 = [shift(r1[half], axes[half][1], 1) for half in range(2)]
    f2 = [shift(l2[half], axes[half][1], -1) for half in range(2)]
    state = run(2, list(zip(r2, l2)), state)
    return run(3, list(zip(f1, f2)), state)


def solution(mesh):
    return jax.shard_map(
        on_device,
        mesh=mesh,
        in_specs=(
            P(None, "pipe", "head"),
            P(("pipe", "head"), None),
            P(("pipe", "head"), None),
            P(),
        ),
        out_specs=P(None, "pipe", "head"),
        check_vma=False,
    )
```

```python
import functools
import math

import jax
import jax.numpy as jnp
from jax import lax
from jax.experimental import pallas as pl
from jax.experimental.pallas import tpu as pltpu
from jax.sharding import PartitionSpec as P

HEAD_SIZE = 128
SCALE = HEAD_SIZE ** -0.5 * math.log2(math.e)
NEG = -1e30
UNIT = 512
PIECE = 64
GROUP = UNIT // PIECE
PEAK_ROW = HEAD_SIZE + 8
STATE_ROWS = PEAK_ROW + 8
WIDE = 4
LARGE = 2.0**100
COLUMNS = 512
VMEM_LIMIT = 36 * 2**20


def pack_body(key_ref, value_ref, out_ref):
    for head in range(4):
        for half in range(2):
            column = (head * 2 + half) * HEAD_SIZE
            lanes = slice(column, column + HEAD_SIZE)
            for to in (head, head + 4):
                out_ref[to, half, 0] = key_ref[:, lanes]
                out_ref[to, half, 1] = value_ref[:, lanes]


def pack(keys, values):
    return pl.pallas_call(
        pack_body,
        in_specs=[pl.BlockSpec(memory_space=pltpu.VMEM)] * 2,
        out_specs=pl.BlockSpec(memory_space=pltpu.VMEM),
        out_shape=jax.ShapeDtypeStruct(
            (GROUP, 2, 2, keys.shape[0], HEAD_SIZE), keys.dtype
        ),
        name="pack",
    )(keys, values)


def prepare_body(query_ref, out_ref, *, length):
    for g in range(query_ref.shape[2] // HEAD_SIZE):
        query = query_ref[0, :, g * HEAD_SIZE : (g + 1) * HEAD_SIZE]
        scaled = query.astype(jnp.float32).T * SCALE
        high = scaled.astype(jnp.bfloat16)
        low = (scaled - high.astype(jnp.float32)).astype(jnp.bfloat16)
        out_ref[:HEAD_SIZE, g * length : (g + 1) * length] = high
        out_ref[HEAD_SIZE:, g * length : (g + 1) * length] = low


def prepare(queries):
    ticks, length, columns = queries.shape
    rows = columns // 2 // HEAD_SIZE * length
    return pl.pallas_call(
        functools.partial(prepare_body, length=length),
        grid=(ticks, 2),
        in_specs=[pl.BlockSpec((1, length, columns // 2), lambda t, h: (t, 0, h))],
        out_specs=pl.BlockSpec(
            (None, None, 2 * HEAD_SIZE, rows), lambda t, h: (t, h, 0, 0)
        ),
        out_shape=jax.ShapeDtypeStruct(
            (ticks, 2, 2 * HEAD_SIZE, rows), jnp.bfloat16
        ),
        compiler_params=pltpu.CompilerParams(vmem_limit_bytes=VMEM_LIMIT),
        name="prepare",
        cost_estimate=pl.CostEstimate(flops=0, bytes_accessed=6 * 2**20, transcendentals=0),
    )(queries)


def attend_body(slices, *refs, units, places, earlier, length, first, last):
    refs = list(refs)
    query_ref = refs.pop(0)
    blocks = [[refs.pop(0) for _ in units[0]], [refs.pop(0) for _ in units[1]]]
    before = None if first else refs.pop(0)
    out_ref = refs.pop(0)
    state, key_buf, value_buf = refs if last else [out_ref] + refs
    count = sum(units[0])
    half, tick = pl.program_id(0), pl.program_id(1)
    rows = query_ref.shape[1]
    pipe = lax.axis_index("pipe")

    def numbered(listed):
        return [
            (((pipe >> 3) + dz) & 3) * 4 + (((pipe >> 1) + dy) & 3)
            for dz, dy in listed
        ]

    ids = [numbered(listed) for listed in places]

    def lanes_of(slot):
        return pl.ds(pl.multiple_of((slot & (WIDE - 1)) * UNIT, UNIT), UNIT)

    for which in range(2):

        @pl.when((half == which) & (tick == 0))
        def _(which=which):
            at = 0
            for block, many in zip(blocks[which], units[which]):
                for j in range(many):
                    slot = sum(
                        jnp.where(other < ids[which][at], 1, 0) for other in ids[which]
                    )
                    key_buf[slot] = block[j, :, 0].reshape(UNIT, HEAD_SIZE)
                    value_buf[slot // WIDE, :, lanes_of(slot)] = (
                        block[j, :, 1].reshape(UNIT, HEAD_SIZE).T
                    )
                    at += 1

    where = slices[tick, pipe]
    seen, final = jnp.int32(0), jnp.int32(0)
    for one, other in zip(*ids):
        unit = jnp.where(half == 0, one, other)
        visible = unit * UNIT <= where * length
        seen += jnp.where(visible, 1, 0)
        final = jnp.maximum(final, jnp.where(visible, unit, 0))
    lead = where * length - final * UNIT
    blank = seen > 0
    for one, other in zip(*[numbered(listed) for listed in earlier]):
        blank &= jnp.where(half == 0, one, other) * UNIT > where * length

    def scores(keys):
        return jnp.dot(
            jnp.concatenate([keys, keys], axis=1),
            query_ref[...],
            preferred_element_type=jnp.float32,
        )

    def mask(value, reach):
        key_at = lax.broadcasted_iota(jnp.int32, value.shape, 0)
        query_at = lax.broadcasted_iota(jnp.int32, value.shape, 1) & (length - 1)
        return jnp.where(key_at - query_at <= reach, value, NEG)

    def with_peak():
        value = mask(scores(key_buf[seen - 1, :16]), lead)
        peak = jnp.max(value, axis=0, keepdims=True)
        state[PEAK_ROW:] = jnp.broadcast_to(peak, (8, rows))

    def add(slot, many, reach=None, at=0):
        keys = key_buf[pl.ds(slot, many)].reshape(many * UNIT, HEAD_SIZE)
        keys = jnp.concatenate([keys, keys], axis=1)
        lanes = pl.ds(pl.multiple_of(at * UNIT, UNIT), many * UNIT)
        values = value_buf[slot // WIDE, :, lanes]
        for column in range(0, rows, COLUMNS):
            here = slice(column, column + COLUMNS)
            value = jnp.dot(
                keys, query_ref[:, here], preferred_element_type=jnp.float32
            )
            if reach is not None:
                value = mask(value, reach)
            weights = jnp.exp2(value - state[PEAK_ROW : PEAK_ROW + 1, here])
            state[HEAD_SIZE:PEAK_ROW, here] += jnp.sum(
                weights.reshape(-1, 8, COLUMNS), axis=0
            )
            state[:HEAD_SIZE, here] += jnp.dot(
                values,
                weights.astype(jnp.bfloat16),
                preferred_element_type=jnp.float32,
            )

    def exact(slot, carry):
        reach = jnp.where(slot == seen - 1, lead, UNIT)
        value = mask(scores(key_buf[slot]), reach)
        old = state[PEAK_ROW : PEAK_ROW + 1, :]
        peak = jnp.maximum(old, jnp.max(value, axis=0, keepdims=True))
        weights = jnp.exp2(value - peak)
        part = jnp.dot(
            value_buf[slot // WIDE, :, lanes_of(slot)],
            weights.astype(jnp.bfloat16),
            preferred_element_type=jnp.float32,
        )
        factor = jnp.exp2(old - peak)
        state[:HEAD_SIZE] = state[:HEAD_SIZE] * factor + part
        total = jnp.sum(weights.reshape(-1, 8, rows), axis=0)
        state[HEAD_SIZE:PEAK_ROW] = state[HEAD_SIZE:PEAK_ROW] * factor + total
        state[PEAK_ROW:] = jnp.broadcast_to(peak, (8, rows))
        return carry

    def start():
        if first:
            state[:PEAK_ROW] = jnp.zeros((PEAK_ROW, rows), jnp.float32)
            state[PEAK_ROW:] = jnp.full((8, rows), NEG, jnp.float32)
        else:
            state[...] = before[...]

    start()
    pl.when(blank)(with_peak)
    whole = jnp.where(lead < UNIT, jnp.maximum(seen - 1, 0), seen)

    def wide(i, carry):
        add(i * WIDE, WIDE)
        return carry

    if count >= WIDE:
        lax.fori_loop(0, whole // WIDE, wide, 0)

    if count > 2:

        @pl.when((whole & 2) != 0)
        def _():
            slot = whole // WIDE * WIDE
            add(slot, 2)

    tail = seen - whole // 2 * 2

    @pl.when(tail == 1)
    def _():
        add(seen - 1, 1, lead, (seen - 1) & 2)

    if count > 1:

        @pl.when(tail == 2)
        def _():
            add(seen - 2, 2, lead + UNIT, (seen - 2) & 2)

    @pl.when(jnp.logical_not(jnp.max(state[HEAD_SIZE:PEAK_ROW]) < LARGE))
    def _():
        start()
        lax.fori_loop(0, seen, exact, 0)

    if last:
        for g in range(rows // length):
            columns = slice(g * length, (g + 1) * length)
            total = jnp.sum(state[HEAD_SIZE:PEAK_ROW, columns], axis=0, keepdims=True)
            result = (state[:HEAD_SIZE, columns] * (1.0 / total)).astype(jnp.bfloat16)
            out_ref[0, :, g * HEAD_SIZE : (g + 1) * HEAD_SIZE] = result.T


def attend(slices, query, blocks, places, earlier, before, length, last):
    ticks, _, depth, rows = query.shape
    units = tuple(tuple(b.shape[0] for b in half) for half in blocks)
    count = sum(units[0])
    flat = [*blocks[0], *blocks[1]]
    first = before is None
    state_spec = pl.BlockSpec((None, None, STATE_ROWS, rows), lambda h, t: (t, h, 0, 0))
    state_shape = (ticks, 2, STATE_ROWS, rows)
    in_specs = [
        pl.BlockSpec(memory_space=pltpu.SMEM),
        pl.BlockSpec((None, None, depth, rows), lambda h, t: (t, h, 0, 0)),
    ]
    in_specs += [pl.BlockSpec(memory_space=pltpu.VMEM)] * len(flat)
    args = [slices, query, *flat]
    if not first:
        in_specs.append(state_spec)
        args.append(before)
    scratch = [
        pltpu.VMEM((count, UNIT, HEAD_SIZE), jnp.bfloat16),
        pltpu.VMEM((-(-count // WIDE), HEAD_SIZE, WIDE * UNIT), jnp.bfloat16),
    ]
    if last:
        group = rows // length
        out_specs = pl.BlockSpec((1, length, group * HEAD_SIZE), lambda h, t: (t, 0, h))
        out_shape = jax.ShapeDtypeStruct(
            (ticks, length, 2 * group * HEAD_SIZE), jnp.bfloat16
        )
        scratch = [pltpu.VMEM((STATE_ROWS, rows), jnp.float32)] + scratch
    else:
        out_specs = state_spec
        out_shape = jax.ShapeDtypeStruct(state_shape, jnp.float32)
    return pl.pallas_call(
        functools.partial(
            attend_body,
            units=units,
            places=places,
            earlier=earlier,
            length=length,
            first=first,
            last=last,
        ),
        grid=(2, ticks),
        in_specs=in_specs,
        out_specs=out_specs,
        out_shape=out_shape,
        scratch_shapes=scratch,
        compiler_params=pltpu.CompilerParams(vmem_limit_bytes=VMEM_LIMIT),
        cost_estimate=pl.CostEstimate(
            flops=2 * ticks * count * UNIT * rows * 2 * HEAD_SIZE * 2,
            bytes_accessed=16 * 2**20,
            transcendentals=2 * ticks * count * UNIT * rows,
        ),
        name=f"attend_{count}",
    )(*args)


def on_device(queries, keys, values, slice_index):
    length = queries.shape[1]
    groups = [list(range(i, i + GROUP)) for i in range(0, 32 * 4, GROUP)]
    both = lax.all_to_all(
        pack(keys, values),
        ("pipe", "head"),
        split_axis=0,
        concat_axis=0,
        axis_index_groups=groups,
        tiled=True,
    )
    query = prepare(queries)

    def shift(x, dim, step):
        stride = 8 if dim == "z" else 2
        table = []
        for i in range(32):
            at = (i // stride) % 4
            table.append((i, i + ((at + step) % 4 - at) * stride))
        return lax.ppermute(x, "pipe", table)

    axes = (("y", "z"), ("z", "y"))
    own = [both[:, half] for half in range(2)]
    right = [shift(own[half], axes[half][0], 1) for half in range(2)]
    left = [shift(own[half], axes[half][0], -1) for half in range(2)]
    opposite = [shift(own[half], axes[half][0], 2) for half in range(2)]
    c1 = [jnp.stack([own[half], right[half]]) for half in range(2)]
    r1 = [shift(c1[half], axes[half][1], 1) for half in range(2)]
    l1 = [shift(c1[half], axes[half][1], -1) for half in range(2)]

    p1, p2 = [(0, 0), (0, -1)], [(0, 1), (0, 2)]
    places = (
        p1 + p2,
        [(f, n) for f in (-1, 1) for _, n in p1],
        [(f, n) for f in (-1, 1) for _, n in p2],
        [(2, n) for _, n in p1 + p2],
    )
    places = [([(f, n) for f, n in p], [(n, f) for f, n in p]) for p in places]

    def run(at, blocks, before):
        earlier = [sum((p[half] for p in places[:at]), []) for half in range(2)]
        return attend(
            slice_index, query, blocks, places[at], earlier, before, length, at == 3
        )

    blocks = [(c1[h], left[h][None], opposite[h][None]) for h in range(2)]
    state = run(0, blocks, None)
    left, opposite, state = lax.optimization_barrier((left, opposite, state))
    c2 = [jnp.stack([left[half], opposite[half]]) for half in range(2)]
    r2 = [shift(c2[half], axes[half][1], 1) for half in range(2)]
    l2 = [shift(c2[half], axes[half][1], -1) for half in range(2)]
    state = run(1, list(zip(r1, l1)), state)
    r1, r2, l2, state = lax.optimization_barrier((r1, r2, l2, state))
    f1 = [shift(r1[half], axes[half][1], 1) for half in range(2)]
    f2 = [shift(l2[half], axes[half][1], -1) for half in range(2)]
    state = run(2, list(zip(r2, l2)), state)
    return run(3, list(zip(f1, f2)), state)


def solution(mesh):
    return jax.shard_map(
        on_device,
        mesh=mesh,
        in_specs=(
            P(None, "pipe", "head"),
            P(("pipe", "head"), None),
            P(("pipe", "head"), None),
            P(),
        ),
        out_specs=P(None, "pipe", "head"),
        check_vma=False,
    )
```

```python
import functools
import math

import jax
import jax.numpy as jnp
from jax import lax
from jax.experimental import pallas as pl
from jax.experimental.pallas import tpu as pltpu
from jax.sharding import PartitionSpec as P

HEAD_SIZE = 128
SCALE = HEAD_SIZE ** -0.5 * math.log2(math.e)
NEG = -1e30
UNIT = 512
PIECE = 64
GROUP = UNIT // PIECE
PEAK_ROW = HEAD_SIZE + 8
STATE_ROWS = PEAK_ROW + 8
WIDE = 4
LARGE = 2.0**100
COLUMNS = 512
VMEM_LIMIT = 36 * 2**20


def pack_body(key_ref, value_ref, out_ref):
    for head in range(4):
        for half in range(2):
            column = (head * 2 + half) * HEAD_SIZE
            lanes = slice(column, column + HEAD_SIZE)
            for to in (head, head + 4):
                out_ref[to, half, 0] = key_ref[:, lanes]
                out_ref[to, half, 1] = value_ref[:, lanes]


def pack(keys, values):
    return pl.pallas_call(
        pack_body,
        in_specs=[pl.BlockSpec(memory_space=pltpu.VMEM)] * 2,
        out_specs=pl.BlockSpec(memory_space=pltpu.VMEM),
        out_shape=jax.ShapeDtypeStruct(
            (GROUP, 2, 2, keys.shape[0], HEAD_SIZE), keys.dtype
        ),
        name="pack",
    )(keys, values)


def prepare_body(query_ref, out_ref, *, length):
    for g in range(query_ref.shape[2] // HEAD_SIZE):
        query = query_ref[0, :, g * HEAD_SIZE : (g + 1) * HEAD_SIZE]
        scaled = query.astype(jnp.float32).T * SCALE
        high = scaled.astype(jnp.bfloat16)
        low = (scaled - high.astype(jnp.float32)).astype(jnp.bfloat16)
        out_ref[:HEAD_SIZE, g * length : (g + 1) * length] = high
        out_ref[HEAD_SIZE:, g * length : (g + 1) * length] = low


def prepare(queries):
    ticks, length, columns = queries.shape
    rows = columns // 2 // HEAD_SIZE * length
    return pl.pallas_call(
        functools.partial(prepare_body, length=length),
        grid=(ticks, 2),
        in_specs=[pl.BlockSpec((1, length, columns // 2), lambda t, h: (t, 0, h))],
        out_specs=pl.BlockSpec(
            (None, None, 2 * HEAD_SIZE, rows), lambda t, h: (t, h, 0, 0)
        ),
        out_shape=jax.ShapeDtypeStruct(
            (ticks, 2, 2 * HEAD_SIZE, rows), jnp.bfloat16
        ),
        compiler_params=pltpu.CompilerParams(vmem_limit_bytes=VMEM_LIMIT),
        name="prepare",
        cost_estimate=pl.CostEstimate(flops=0, bytes_accessed=6 * 2**20, transcendentals=0),
    )(queries)


def attend_body(slices, *refs, units, places, earlier, length, first, last):
    refs = list(refs)
    query_ref = refs.pop(0)
    blocks = [[refs.pop(0) for _ in units[0]], [refs.pop(0) for _ in units[1]]]
    before = None if first else refs.pop(0)
    out_ref = refs.pop(0)
    state, key_buf, value_buf = refs if last else [out_ref] + refs
    count = sum(units[0])
    half, tick = pl.program_id(0), pl.program_id(1)
    rows = query_ref.shape[1]
    pipe = lax.axis_index("pipe")

    def numbered(listed):
        return [
            (((pipe >> 3) + dz) & 3) * 4 + (((pipe >> 1) + dy) & 3)
            for dz, dy in listed
        ]

    ids = [numbered(listed) for listed in places]

    def lanes_of(slot):
        return pl.ds(pl.multiple_of((slot & (WIDE - 1)) * UNIT, UNIT), UNIT)

    for which in range(2):

        @pl.when((half == which) & (tick == 0))
        def _(which=which):
            at = 0
            for block, many in zip(blocks[which], units[which]):
                for j in range(many):
                    slot = sum(
                        jnp.where(other < ids[which][at], 1, 0) for other in ids[which]
                    )
                    key_buf[slot] = block[j, :, 0].reshape(UNIT, HEAD_SIZE)
                    value_buf[slot // WIDE, :, lanes_of(slot)] = (
                        block[j, :, 1].reshape(UNIT, HEAD_SIZE).T
                    )
                    at += 1

    where = slices[tick, pipe]
    seen, final = jnp.int32(0), jnp.int32(0)
    for one, other in zip(*ids):
        unit = jnp.where(half == 0, one, other)
        visible = unit * UNIT <= where * length
        seen += jnp.where(visible, 1, 0)
        final = jnp.maximum(final, jnp.where(visible, unit, 0))
    lead = where * length - final * UNIT
    blank = seen > 0
    for one, other in zip(*[numbered(listed) for listed in earlier]):
        blank &= jnp.where(half == 0, one, other) * UNIT > where * length

    def scores(keys):
        return jnp.dot(
            jnp.concatenate([keys, keys], axis=1),
            query_ref[...],
            preferred_element_type=jnp.float32,
        )

    def mask(value, reach):
        key_at = lax.broadcasted_iota(jnp.int32, value.shape, 0)
        query_at = lax.broadcasted_iota(jnp.int32, value.shape, 1) & (length - 1)
        return jnp.where(key_at - query_at <= reach, value, NEG)

    def with_peak():
        value = mask(scores(key_buf[seen - 1, :16]), lead)
        peak = jnp.max(value, axis=0, keepdims=True)
        state[PEAK_ROW:] = jnp.broadcast_to(peak, (8, rows))

    def add(slot, many, reach=None, at=0):
        keys = key_buf[pl.ds(slot, many)].reshape(many * UNIT, HEAD_SIZE)
        keys = jnp.concatenate([keys, keys], axis=1)
        lanes = pl.ds(pl.multiple_of(at * UNIT, UNIT), many * UNIT)
        values = value_buf[slot // WIDE, :, lanes]
        for column in range(0, rows, COLUMNS):
            here = slice(column, column + COLUMNS)
            value = jnp.dot(
                keys, query_ref[:, here], preferred_element_type=jnp.float32
            )
            if reach is not None:
                value = mask(value, reach)
            weights = jnp.exp2(value - state[PEAK_ROW : PEAK_ROW + 1, here])
            state[HEAD_SIZE:PEAK_ROW, here] += jnp.sum(
                weights.reshape(-1, 8, COLUMNS), axis=0
            )
            state[:HEAD_SIZE, here] += jnp.dot(
                values,
                weights.astype(jnp.bfloat16),
                preferred_element_type=jnp.float32,
            )

    def exact(slot, carry):
        reach = jnp.where(slot == seen - 1, lead, UNIT)
        value = mask(scores(key_buf[slot]), reach)
        old = state[PEAK_ROW : PEAK_ROW + 1, :]
        peak = jnp.maximum(old, jnp.max(value, axis=0, keepdims=True))
        weights = jnp.exp2(value - peak)
        part = jnp.dot(
            value_buf[slot // WIDE, :, lanes_of(slot)],
            weights.astype(jnp.bfloat16),
            preferred_element_type=jnp.float32,
        )
        factor = jnp.exp2(old - peak)
        state[:HEAD_SIZE] = state[:HEAD_SIZE] * factor + part
        total = jnp.sum(weights.reshape(-1, 8, rows), axis=0)
        state[HEAD_SIZE:PEAK_ROW] = state[HEAD_SIZE:PEAK_ROW] * factor + total
        state[PEAK_ROW:] = jnp.broadcast_to(peak, (8, rows))
        return carry

    def start():
        if first:
            state[:PEAK_ROW] = jnp.zeros((PEAK_ROW, rows), jnp.float32)
            state[PEAK_ROW:] = jnp.full((8, rows), NEG, jnp.float32)
        else:
            state[...] = before[...]

    start()
    pl.when(blank)(with_peak)
    whole = jnp.where(lead < UNIT, jnp.maximum(seen - 1, 0), seen)

    def wide(i, carry):
        add(i * WIDE, WIDE)
        return carry

    if count >= WIDE:
        lax.fori_loop(0, whole // WIDE, wide, 0)

    if count > 2:

        @pl.when((whole & 2) != 0)
        def _():
            slot = whole // WIDE * WIDE
            add(slot, 2)

    tail = seen - whole // 2 * 2

    @pl.when(tail == 1)
    def _():
        add(seen - 1, 1, lead, (seen - 1) & 2)

    if count > 1:

        @pl.when(tail == 2)
        def _():
            add(seen - 2, 2, lead + UNIT, (seen - 2) & 2)

    @pl.when(jnp.logical_not(jnp.max(state[HEAD_SIZE:PEAK_ROW]) < LARGE))
    def _():
        start()
        lax.fori_loop(0, seen, exact, 0)

    if last:
        for g in range(rows // length):
            columns = slice(g * length, (g + 1) * length)
            total = jnp.sum(state[HEAD_SIZE:PEAK_ROW, columns], axis=0, keepdims=True)
            result = (state[:HEAD_SIZE, columns] * (1.0 / total)).astype(jnp.bfloat16)
            out_ref[0, :, g * HEAD_SIZE : (g + 1) * HEAD_SIZE] = result.T


def attend(slices, query, blocks, places, earlier, before, length, last):
    ticks, _, depth, rows = query.shape
    units = tuple(tuple(b.shape[0] for b in half) for half in blocks)
    count = sum(units[0])
    flat = [*blocks[0], *blocks[1]]
    first = before is None
    state_spec = pl.BlockSpec((None, None, STATE_ROWS, rows), lambda h, t: (t, h, 0, 0))
    state_shape = (ticks, 2, STATE_ROWS, rows)
    in_specs = [
        pl.BlockSpec(memory_space=pltpu.SMEM),
        pl.BlockSpec((None, None, depth, rows), lambda h, t: (t, h, 0, 0)),
    ]
    in_specs += [pl.BlockSpec(memory_space=pltpu.VMEM)] * len(flat)
    args = [slices, query, *flat]
    if not first:
        in_specs.append(state_spec)
        args.append(before)
    scratch = [
        pltpu.VMEM((count, UNIT, HEAD_SIZE), jnp.bfloat16),
        pltpu.VMEM((-(-count // WIDE), HEAD_SIZE, WIDE * UNIT), jnp.bfloat16),
    ]
    if last:
        group = rows // length
        out_specs = pl.BlockSpec((1, length, group * HEAD_SIZE), lambda h, t: (t, 0, h))
        out_shape = jax.ShapeDtypeStruct(
            (ticks, length, 2 * group * HEAD_SIZE), jnp.bfloat16
        )
        scratch = [pltpu.VMEM((STATE_ROWS, rows), jnp.float32)] + scratch
    else:
        out_specs = state_spec
        out_shape = jax.ShapeDtypeStruct(state_shape, jnp.float32)
    return pl.pallas_call(
        functools.partial(
            attend_body,
            units=units,
            places=places,
            earlier=earlier,
            length=length,
            first=first,
            last=last,
        ),
        grid=(2, ticks),
        in_specs=in_specs,
        out_specs=out_specs,
        out_shape=out_shape,
        scratch_shapes=scratch,
        compiler_params=pltpu.CompilerParams(vmem_limit_bytes=VMEM_LIMIT),
        cost_estimate=pl.CostEstimate(
            flops=2 * ticks * count * UNIT * rows * 2 * HEAD_SIZE * 2,
            bytes_accessed=16 * 2**20,
            transcendentals=2 * ticks * count * UNIT * rows,
        ),
        name=f"attend_{count}",
    )(*args)


def on_device(queries, keys, values, slice_index):
    length = queries.shape[1]
    groups = [list(range(i, i + GROUP)) for i in range(0, 32 * 4, GROUP)]
    both = lax.all_to_all(
        pack(keys, values),
        ("pipe", "head"),
        split_axis=0,
        concat_axis=0,
        axis_index_groups=groups,
        tiled=True,
    )
    query = prepare(queries)

    def shift(x, dim, step):
        stride = 8 if dim == "z" else 2
        table = []
        for i in range(32):
            at = (i // stride) % 4
            table.append((i, i + ((at + step) % 4 - at) * stride))
        return lax.ppermute(x, "pipe", table)

    axes = (("y", "z"), ("z", "y"))
    own = [both[:, half] for half in range(2)]
    near = [
        [shift(own[half], axes[half][0], step) for half in range(2)]
        for step in (1, -1, 2)
    ]
    held = [jnp.stack([own[half], *(n[half] for n in near)]) for half in range(2)]
    right = [shift(held[half], axes[half][1], 1) for half in range(2)]
    left = [shift(held[half], axes[half][1], -1) for half in range(2)]

    listed = [(0, 0), (0, -1), (0, 1), (0, 2)]
    places = (
        listed,
        [(f, n) for f in (-1, 1) for _, n in listed],
        [(2, n) for _, n in listed],
    )
    places = [([(f, n) for f, n in p], [(n, f) for f, n in p]) for p in places]

    def run(at, blocks, before):
        earlier = [sum((p[half] for p in places[:at]), []) for half in range(2)]
        return attend(
            slice_index, query, blocks, places[at], earlier, before, length, at == 2
        )

    state = run(0, [(held[half],) for half in range(2)], None)
    right, left, state = lax.optimization_barrier((right, left, state))
    middle = len(listed) // 2
    far = [
        (
            shift(right[half][:middle], axes[half][1], 1),
            shift(left[half][middle:], axes[half][1], -1),
        )
        for half in range(2)
    ]
    state = run(1, list(zip(right, left)), state)
    return run(2, far, state)


def solution(mesh):
    return jax.shard_map(
        on_device,
        mesh=mesh,
        in_specs=(
            P(None, "pipe", "head"),
            P(("pipe", "head"), None),
            P(("pipe", "head"), None),
            P(),
        ),
        out_specs=P(None, "pipe", "head"),
        check_vma=False,
    )
```

```python
import functools
import math

import jax
import jax.numpy as jnp
from jax import lax
from jax.experimental import pallas as pl
from jax.experimental.pallas import tpu as pltpu
from jax.sharding import PartitionSpec as P

HEAD_SIZE = 128
SCALE = HEAD_SIZE ** -0.5 * math.log2(math.e)
NEG = -1e30
UNIT = 512
PIECE = 64
GROUP = UNIT // PIECE
PEAK_ROW = HEAD_SIZE + 8
STATE_ROWS = PEAK_ROW + 8
WIDE = 4
LARGE = 2.0**100
COLUMNS = 512
VMEM_LIMIT = 36 * 2**20


def pack_body(key_ref, value_ref, out_ref):
    for head in range(4):
        for half in range(2):
            column = (head * 2 + half) * HEAD_SIZE
            lanes = slice(column, column + HEAD_SIZE)
            for to in (head, head + 4):
                out_ref[to, half, 0] = key_ref[:, lanes]
                out_ref[to, half, 1] = value_ref[:, lanes]


def pack(keys, values):
    return pl.pallas_call(
        pack_body,
        in_specs=[pl.BlockSpec(memory_space=pltpu.VMEM)] * 2,
        out_specs=pl.BlockSpec(memory_space=pltpu.VMEM),
        out_shape=jax.ShapeDtypeStruct(
            (GROUP, 2, 2, keys.shape[0], HEAD_SIZE), keys.dtype
        ),
        name="pack",
    )(keys, values)


def prepare_body(query_ref, out_ref, *, length):
    for g in range(query_ref.shape[2] // HEAD_SIZE):
        query = query_ref[0, :, g * HEAD_SIZE : (g + 1) * HEAD_SIZE]
        scaled = query.astype(jnp.float32).T * SCALE
        high = scaled.astype(jnp.bfloat16)
        low = (scaled - high.astype(jnp.float32)).astype(jnp.bfloat16)
        out_ref[:HEAD_SIZE, g * length : (g + 1) * length] = high
        out_ref[HEAD_SIZE:, g * length : (g + 1) * length] = low


def prepare(queries):
    ticks, length, columns = queries.shape
    rows = columns // 2 // HEAD_SIZE * length
    return pl.pallas_call(
        functools.partial(prepare_body, length=length),
        grid=(ticks, 2),
        in_specs=[pl.BlockSpec((1, length, columns // 2), lambda t, h: (t, 0, h))],
        out_specs=pl.BlockSpec(
            (None, None, 2 * HEAD_SIZE, rows), lambda t, h: (t, h, 0, 0)
        ),
        out_shape=jax.ShapeDtypeStruct(
            (ticks, 2, 2 * HEAD_SIZE, rows), jnp.bfloat16
        ),
        compiler_params=pltpu.CompilerParams(vmem_limit_bytes=VMEM_LIMIT),
        name="prepare",
        cost_estimate=pl.CostEstimate(flops=0, bytes_accessed=6 * 2**20, transcendentals=0),
    )(queries)


def attend_body(slices, *refs, units, places, earlier, length, first, last):
    refs = list(refs)
    query_ref = refs.pop(0)
    blocks = [[refs.pop(0) for _ in units[0]], [refs.pop(0) for _ in units[1]]]
    before = None if first else refs.pop(0)
    out_ref = refs.pop(0)
    state, key_buf, value_buf = refs if last else [out_ref] + refs
    count = sum(units[0])
    half, tick = pl.program_id(0), pl.program_id(1)
    rows = query_ref.shape[1]
    pipe = lax.axis_index("pipe")

    def numbered(listed):
        return [
            (((pipe >> 3) + dz) & 3) * 4 + (((pipe >> 1) + dy) & 3)
            for dz, dy in listed
        ]

    ids = [numbered(listed) for listed in places]

    def lanes_of(slot):
        return pl.ds(pl.multiple_of((slot & (WIDE - 1)) * UNIT, UNIT), UNIT)

    for which in range(2):

        @pl.when((half == which) & (tick == 0))
        def _(which=which):
            at = 0
            for block, many in zip(blocks[which], units[which]):
                for j in range(many):
                    slot = sum(
                        jnp.where(other < ids[which][at], 1, 0) for other in ids[which]
                    )
                    key_buf[slot] = block[j, :, 0].reshape(UNIT, HEAD_SIZE)
                    value_buf[slot // WIDE, :, lanes_of(slot)] = (
                        block[j, :, 1].reshape(UNIT, HEAD_SIZE).T
                    )
                    at += 1

    where = slices[tick, pipe]
    seen, final = jnp.int32(0), jnp.int32(0)
    for one, other in zip(*ids):
        unit = jnp.where(half == 0, one, other)
        visible = unit * UNIT <= where * length
        seen += jnp.where(visible, 1, 0)
        final = jnp.maximum(final, jnp.where(visible, unit, 0))
    lead = where * length - final * UNIT
    blank = seen > 0
    for one, other in zip(*[numbered(listed) for listed in earlier]):
        blank &= jnp.where(half == 0, one, other) * UNIT > where * length

    def scores(keys):
        return jnp.dot(
            jnp.concatenate([keys, keys], axis=1),
            query_ref[...],
            preferred_element_type=jnp.float32,
        )

    def mask(value, reach):
        key_at = lax.broadcasted_iota(jnp.int32, value.shape, 0)
        query_at = lax.broadcasted_iota(jnp.int32, value.shape, 1) & (length - 1)
        return jnp.where(key_at - query_at <= reach, value, NEG)

    def with_peak():
        value = mask(scores(key_buf[seen - 1, :16]), lead)
        peak = jnp.max(value, axis=0, keepdims=True)
        state[PEAK_ROW:] = jnp.broadcast_to(peak, (8, rows))

    def add(slot, many, reach=None, at=0):
        keys = key_buf[pl.ds(slot, many)].reshape(many * UNIT, HEAD_SIZE)
        keys = jnp.concatenate([keys, keys], axis=1)
        lanes = pl.ds(pl.multiple_of(at * UNIT, UNIT), many * UNIT)
        values = value_buf[slot // WIDE, :, lanes]
        for column in range(0, rows, COLUMNS):
            here = slice(column, column + COLUMNS)
            value = jnp.dot(
                keys, query_ref[:, here], preferred_element_type=jnp.float32
            )
            if reach is not None:
                value = mask(value, reach)
            weights = jnp.exp2(value - state[PEAK_ROW : PEAK_ROW + 1, here])
            state[HEAD_SIZE:PEAK_ROW, here] += jnp.sum(
                weights.reshape(-1, 8, COLUMNS), axis=0
            )
            state[:HEAD_SIZE, here] += jnp.dot(
                values,
                weights.astype(jnp.bfloat16),
                preferred_element_type=jnp.float32,
            )

    def exact(slot, carry):
        reach = jnp.where(slot == seen - 1, lead, UNIT)
        value = mask(scores(key_buf[slot]), reach)
        old = state[PEAK_ROW : PEAK_ROW + 1, :]
        peak = jnp.maximum(old, jnp.max(value, axis=0, keepdims=True))
        weights = jnp.exp2(value - peak)
        part = jnp.dot(
            value_buf[slot // WIDE, :, lanes_of(slot)],
            weights.astype(jnp.bfloat16),
            preferred_element_type=jnp.float32,
        )
        factor = jnp.exp2(old - peak)
        state[:HEAD_SIZE] = state[:HEAD_SIZE] * factor + part
        total = jnp.sum(weights.reshape(-1, 8, rows), axis=0)
        state[HEAD_SIZE:PEAK_ROW] = state[HEAD_SIZE:PEAK_ROW] * factor + total
        state[PEAK_ROW:] = jnp.broadcast_to(peak, (8, rows))
        return carry

    def start():
        if first:
            state[:PEAK_ROW] = jnp.zeros((PEAK_ROW, rows), jnp.float32)
            state[PEAK_ROW:] = jnp.full((8, rows), NEG, jnp.float32)
        else:
            state[...] = before[...]

    start()
    pl.when(blank)(with_peak)
    whole = jnp.where(lead < UNIT, jnp.maximum(seen - 1, 0), seen)

    def wide(i, carry):
        add(i * WIDE, WIDE)
        return carry

    if count >= WIDE:
        lax.fori_loop(0, whole // WIDE, wide, 0)

    if count > 2:

        @pl.when((whole & 2) != 0)
        def _():
            slot = whole // WIDE * WIDE
            add(slot, 2)

    tail = seen - whole // 2 * 2

    @pl.when(tail == 1)
    def _():
        add(seen - 1, 1, lead, (seen - 1) & 2)

    if count > 1:

        @pl.when(tail == 2)
        def _():
            add(seen - 2, 2, lead + UNIT, (seen - 2) & 2)

    @pl.when(jnp.logical_not(jnp.max(state[HEAD_SIZE:PEAK_ROW]) < LARGE))
    def _():
        start()
        lax.fori_loop(0, seen, exact, 0)

    if last:
        for g in range(rows // length):
            columns = slice(g * length, (g + 1) * length)
            total = jnp.sum(state[HEAD_SIZE:PEAK_ROW, columns], axis=0, keepdims=True)
            result = (state[:HEAD_SIZE, columns] * (1.0 / total)).astype(jnp.bfloat16)
            out_ref[0, :, g * HEAD_SIZE : (g + 1) * HEAD_SIZE] = result.T


def attend(slices, query, blocks, places, earlier, before, length, last):
    ticks, _, depth, rows = query.shape
    units = tuple(tuple(b.shape[0] for b in half) for half in blocks)
    count = sum(units[0])
    flat = [*blocks[0], *blocks[1]]
    first = before is None
    state_spec = pl.BlockSpec((None, None, STATE_ROWS, rows), lambda h, t: (t, h, 0, 0))
    state_shape = (ticks, 2, STATE_ROWS, rows)
    in_specs = [
        pl.BlockSpec(memory_space=pltpu.SMEM),
        pl.BlockSpec((None, None, depth, rows), lambda h, t: (t, h, 0, 0)),
    ]
    in_specs += [pl.BlockSpec(memory_space=pltpu.VMEM)] * len(flat)
    args = [slices, query, *flat]
    if not first:
        in_specs.append(state_spec)
        args.append(before)
    scratch = [
        pltpu.VMEM((count, UNIT, HEAD_SIZE), jnp.bfloat16),
        pltpu.VMEM((-(-count // WIDE), HEAD_SIZE, WIDE * UNIT), jnp.bfloat16),
    ]
    if last:
        group = rows // length
        out_specs = pl.BlockSpec((1, length, group * HEAD_SIZE), lambda h, t: (t, 0, h))
        out_shape = jax.ShapeDtypeStruct(
            (ticks, length, 2 * group * HEAD_SIZE), jnp.bfloat16
        )
        scratch = [pltpu.VMEM((STATE_ROWS, rows), jnp.float32)] + scratch
    else:
        out_specs = state_spec
        out_shape = jax.ShapeDtypeStruct(state_shape, jnp.float32)
    return pl.pallas_call(
        functools.partial(
            attend_body,
            units=units,
            places=places,
            earlier=earlier,
            length=length,
            first=first,
            last=last,
        ),
        grid=(2, ticks),
        in_specs=in_specs,
        out_specs=out_specs,
        out_shape=out_shape,
        scratch_shapes=scratch,
        compiler_params=pltpu.CompilerParams(vmem_limit_bytes=VMEM_LIMIT),
        cost_estimate=pl.CostEstimate(
            flops=2 * ticks * count * UNIT * rows * 2 * HEAD_SIZE * 2,
            bytes_accessed=16 * 2**20,
            transcendentals=2 * ticks * count * UNIT * rows,
        ),
        name=f"attend_{count}",
    )(*args)


def on_device(queries, keys, values, slice_index):
    length = queries.shape[1]
    groups = [list(range(i, i + GROUP)) for i in range(0, 32 * 4, GROUP)]
    both = lax.all_to_all(
        pack(keys, values),
        ("pipe", "head"),
        split_axis=0,
        concat_axis=0,
        axis_index_groups=groups,
        tiled=True,
    )
    query = prepare(queries)

    def shift(x, dim, step):
        stride = 8 if dim == "z" else 2
        table = []
        for i in range(32):
            at = (i // stride) % 4
            table.append((i, i + ((at + step) % 4 - at) * stride))
        return lax.ppermute(x, "pipe", table)

    axes = (("y", "z"), ("z", "y"))
    own = [both[:, half] for half in range(2)]
    after = [shift(own[half], axes[half][0], -1) for half in range(2)]
    before = [shift(own[half], axes[half][0], 1) for half in range(2)]
    opposite = [shift(after[half], axes[half][0], -1) for half in range(2)]
    before, query = lax.optimization_barrier((before, query))
    held = [
        jnp.stack([own[half], before[half], after[half], opposite[half]])
        for half in range(2)
    ]
    right = [shift(held[half], axes[half][1], 1) for half in range(2)]
    left = [shift(held[half], axes[half][1], -1) for half in range(2)]

    listed = [(0, 0), (0, -1), (0, 1), (0, 2)]
    places = (
        listed,
        [(f, n) for f in (-1, 1) for _, n in listed],
        [(2, n) for _, n in listed],
    )
    places = [([(f, n) for f, n in p], [(n, f) for f, n in p]) for p in places]

    def run(at, blocks, before):
        earlier = [sum((p[half] for p in places[:at]), []) for half in range(2)]
        return attend(
            slice_index, query, blocks, places[at], earlier, before, length, at == 2
        )

    state = run(0, [(held[half],) for half in range(2)], None)
    right, state = lax.optimization_barrier((right, state))
    far = [(shift(right[half], axes[half][1], 1),) for half in range(2)]
    state = run(1, list(zip(right, left)), state)
    return run(2, far, state)


def solution(mesh):
    return jax.shard_map(
        on_device,
        mesh=mesh,
        in_specs=(
            P(None, "pipe", "head"),
            P(("pipe", "head"), None),
            P(("pipe", "head"), None),
            P(),
        ),
        out_specs=P(None, "pipe", "head"),
        check_vma=False,
    )
```

```python
import functools
import math

import jax
import jax.numpy as jnp
from jax import lax
from jax.experimental import pallas as pl
from jax.experimental.pallas import tpu as pltpu
from jax.sharding import PartitionSpec as P

HEAD_SIZE = 128
SCALE = HEAD_SIZE ** -0.5 * math.log2(math.e)
NEG = -1e30
UNIT = 512
PIECE = 64
GROUP = UNIT // PIECE
PEAK_ROW = HEAD_SIZE + 8
STATE_ROWS = PEAK_ROW + 8
WIDE = 4
LARGE = 2.0**100
COLUMNS = 512
VMEM_LIMIT = 36 * 2**20


def pack_body(key_ref, value_ref, out_ref):
    for head in range(4):
        for half in range(2):
            column = (head * 2 + half) * HEAD_SIZE
            lanes = slice(column, column + HEAD_SIZE)
            for to in (head, head + 4):
                out_ref[to, half, 0] = key_ref[:, lanes]
                out_ref[to, half, 1] = value_ref[:, lanes]


def pack(keys, values):
    return pl.pallas_call(
        pack_body,
        in_specs=[pl.BlockSpec(memory_space=pltpu.VMEM)] * 2,
        out_specs=pl.BlockSpec(memory_space=pltpu.VMEM),
        out_shape=jax.ShapeDtypeStruct(
            (GROUP, 2, 2, keys.shape[0], HEAD_SIZE), keys.dtype
        ),
        name="pack",
    )(keys, values)


def prepare_body(query_ref, out_ref, *, length):
    for g in range(query_ref.shape[2] // HEAD_SIZE):
        query = query_ref[0, :, g * HEAD_SIZE : (g + 1) * HEAD_SIZE]
        scaled = query.astype(jnp.float32).T * SCALE
        high = scaled.astype(jnp.bfloat16)
        low = (scaled - high.astype(jnp.float32)).astype(jnp.bfloat16)
        out_ref[:HEAD_SIZE, g * length : (g + 1) * length] = high
        out_ref[HEAD_SIZE:, g * length : (g + 1) * length] = low


def prepare(queries):
    ticks, length, columns = queries.shape
    rows = columns // 2 // HEAD_SIZE * length
    return pl.pallas_call(
        functools.partial(prepare_body, length=length),
        grid=(ticks, 2),
        in_specs=[pl.BlockSpec((1, length, columns // 2), lambda t, h: (t, 0, h))],
        out_specs=pl.BlockSpec(
            (None, None, 2 * HEAD_SIZE, rows), lambda t, h: (t, h, 0, 0)
        ),
        out_shape=jax.ShapeDtypeStruct(
            (ticks, 2, 2 * HEAD_SIZE, rows), jnp.bfloat16
        ),
        compiler_params=pltpu.CompilerParams(vmem_limit_bytes=VMEM_LIMIT),
        name="prepare",
        cost_estimate=pl.CostEstimate(flops=0, bytes_accessed=6 * 2**20, transcendentals=0),
    )(queries)


def attend_body(slices, *refs, units, places, earlier, length, first, last):
    refs = list(refs)
    query_ref = refs.pop(0)
    blocks = [[refs.pop(0) for _ in units[0]], [refs.pop(0) for _ in units[1]]]
    before = None if first else refs.pop(0)
    out_ref = refs.pop(0)
    state, key_buf, value_buf = refs if last else [out_ref] + refs
    count = sum(units[0])
    half, tick = pl.program_id(0), pl.program_id(1)
    rows = query_ref.shape[1]
    pipe = lax.axis_index("pipe")

    def numbered(listed):
        return [
            (((pipe >> 3) + dz) & 3) * 4 + (((pipe >> 1) + dy) & 3)
            for dz, dy in listed
        ]

    ids = [numbered(listed) for listed in places]

    def lanes_of(slot):
        return pl.ds(pl.multiple_of((slot & (WIDE - 1)) * UNIT, UNIT), UNIT)

    for which in range(2):

        @pl.when((half == which) & (tick == 0))
        def _(which=which):
            at = 0
            for block, many in zip(blocks[which], units[which]):
                for j in range(many):
                    slot = sum(
                        jnp.where(other < ids[which][at], 1, 0) for other in ids[which]
                    )
                    key_buf[slot] = block[j, :, 0].reshape(UNIT, HEAD_SIZE)
                    value_buf[slot // WIDE, :, lanes_of(slot)] = (
                        block[j, :, 1].reshape(UNIT, HEAD_SIZE).T
                    )
                    at += 1

    where = slices[tick, pipe]
    seen, final = jnp.int32(0), jnp.int32(0)
    for one, other in zip(*ids):
        unit = jnp.where(half == 0, one, other)
        visible = unit * UNIT <= where * length
        seen += jnp.where(visible, 1, 0)
        final = jnp.maximum(final, jnp.where(visible, unit, 0))
    lead = where * length - final * UNIT
    blank = seen > 0
    for one, other in zip(*[numbered(listed) for listed in earlier]):
        blank &= jnp.where(half == 0, one, other) * UNIT > where * length

    def scores(keys):
        return jnp.dot(
            jnp.concatenate([keys, keys], axis=1),
            query_ref[...],
            preferred_element_type=jnp.float32,
        )

    def mask(value, reach):
        key_at = lax.broadcasted_iota(jnp.int32, value.shape, 0)
        query_at = lax.broadcasted_iota(jnp.int32, value.shape, 1) & (length - 1)
        return jnp.where(key_at - query_at <= reach, value, NEG)

    def with_peak():
        value = mask(scores(key_buf[seen - 1, :16]), lead)
        peak = jnp.max(value, axis=0, keepdims=True)
        state[PEAK_ROW:] = jnp.broadcast_to(peak, (8, rows))

    def add(slot, many, reach=None, at=0):
        keys = key_buf[pl.ds(slot, many)].reshape(many * UNIT, HEAD_SIZE)
        keys = jnp.concatenate([keys, keys], axis=1)
        lanes = pl.ds(pl.multiple_of(at * UNIT, UNIT), many * UNIT)
        values = value_buf[slot // WIDE, :, lanes]
        for column in range(0, rows, COLUMNS):
            here = slice(column, column + COLUMNS)
            value = jnp.dot(
                keys, query_ref[:, here], preferred_element_type=jnp.float32
            )
            if reach is not None:
                value = mask(value, reach)
            weights = jnp.exp2(value - state[PEAK_ROW : PEAK_ROW + 1, here])
            state[HEAD_SIZE:PEAK_ROW, here] += jnp.sum(
                weights.reshape(-1, 8, COLUMNS), axis=0
            )
            state[:HEAD_SIZE, here] += jnp.dot(
                values,
                weights.astype(jnp.bfloat16),
                preferred_element_type=jnp.float32,
            )

    def exact(slot, carry):
        reach = jnp.where(slot == seen - 1, lead, UNIT)
        value = mask(scores(key_buf[slot]), reach)
        old = state[PEAK_ROW : PEAK_ROW + 1, :]
        peak = jnp.maximum(old, jnp.max(value, axis=0, keepdims=True))
        weights = jnp.exp2(value - peak)
        part = jnp.dot(
            value_buf[slot // WIDE, :, lanes_of(slot)],
            weights.astype(jnp.bfloat16),
            preferred_element_type=jnp.float32,
        )
        factor = jnp.exp2(old - peak)
        state[:HEAD_SIZE] = state[:HEAD_SIZE] * factor + part
        total = jnp.sum(weights.reshape(-1, 8, rows), axis=0)
        state[HEAD_SIZE:PEAK_ROW] = state[HEAD_SIZE:PEAK_ROW] * factor + total
        state[PEAK_ROW:] = jnp.broadcast_to(peak, (8, rows))
        return carry

    def start():
        if first:
            state[:PEAK_ROW] = jnp.zeros((PEAK_ROW, rows), jnp.float32)
            state[PEAK_ROW:] = jnp.full((8, rows), NEG, jnp.float32)
        else:
            state[...] = before[...]

    start()
    pl.when(blank)(with_peak)
    whole = jnp.where(lead < UNIT, jnp.maximum(seen - 1, 0), seen)

    def wide(i, carry):
        add(i * WIDE, WIDE)
        return carry

    if count >= WIDE:
        lax.fori_loop(0, whole // WIDE, wide, 0)

    if count > 2:

        @pl.when((whole & 2) != 0)
        def _():
            slot = whole // WIDE * WIDE
            add(slot, 2)

    tail = seen - whole // 2 * 2

    @pl.when(tail == 1)
    def _():
        add(seen - 1, 1, lead, (seen - 1) & 2)

    if count > 1:

        @pl.when(tail == 2)
        def _():
            add(seen - 2, 2, lead + UNIT, (seen - 2) & 2)

    @pl.when(jnp.logical_not(jnp.max(state[HEAD_SIZE:PEAK_ROW]) < LARGE))
    def _():
        start()
        lax.fori_loop(0, seen, exact, 0)

    if last:
        for g in range(rows // length):
            columns = slice(g * length, (g + 1) * length)
            total = jnp.sum(state[HEAD_SIZE:PEAK_ROW, columns], axis=0, keepdims=True)
            result = (state[:HEAD_SIZE, columns] * (1.0 / total)).astype(jnp.bfloat16)
            out_ref[0, :, g * HEAD_SIZE : (g + 1) * HEAD_SIZE] = result.T


def attend(slices, query, blocks, places, earlier, before, length, last):
    ticks, _, depth, rows = query.shape
    units = tuple(tuple(b.shape[0] for b in half) for half in blocks)
    count = sum(units[0])
    flat = [*blocks[0], *blocks[1]]
    first = before is None
    state_spec = pl.BlockSpec((None, None, STATE_ROWS, rows), lambda h, t: (t, h, 0, 0))
    state_shape = (ticks, 2, STATE_ROWS, rows)
    in_specs = [
        pl.BlockSpec(memory_space=pltpu.SMEM),
        pl.BlockSpec((None, None, depth, rows), lambda h, t: (t, h, 0, 0)),
    ]
    in_specs += [pl.BlockSpec(memory_space=pltpu.VMEM)] * len(flat)
    args = [slices, query, *flat]
    if not first:
        in_specs.append(state_spec)
        args.append(before)
    scratch = [
        pltpu.VMEM((count, UNIT, HEAD_SIZE), jnp.bfloat16),
        pltpu.VMEM((-(-count // WIDE), HEAD_SIZE, WIDE * UNIT), jnp.bfloat16),
    ]
    if last:
        group = rows // length
        out_specs = pl.BlockSpec((1, length, group * HEAD_SIZE), lambda h, t: (t, 0, h))
        out_shape = jax.ShapeDtypeStruct(
            (ticks, length, 2 * group * HEAD_SIZE), jnp.bfloat16
        )
        scratch = [pltpu.VMEM((STATE_ROWS, rows), jnp.float32)] + scratch
    else:
        out_specs = state_spec
        out_shape = jax.ShapeDtypeStruct(state_shape, jnp.float32)
    return pl.pallas_call(
        functools.partial(
            attend_body,
            units=units,
            places=places,
            earlier=earlier,
            length=length,
            first=first,
            last=last,
        ),
        grid=(2, ticks),
        in_specs=in_specs,
        out_specs=out_specs,
        out_shape=out_shape,
        scratch_shapes=scratch,
        compiler_params=pltpu.CompilerParams(vmem_limit_bytes=VMEM_LIMIT),
        cost_estimate=pl.CostEstimate(
            flops=2 * ticks * count * UNIT * rows * 2 * HEAD_SIZE * 2,
            bytes_accessed=16 * 2**20,
            transcendentals=2 * ticks * count * UNIT * rows,
        ),
        name=f"attend_{count}",
    )(*args)


def on_device(queries, keys, values, slice_index):
    length = queries.shape[1]
    groups = [list(range(i, i + GROUP)) for i in range(0, 32 * 4, GROUP)]
    both = lax.all_to_all(
        pack(keys, values),
        ("pipe", "head"),
        split_axis=0,
        concat_axis=0,
        axis_index_groups=groups,
        tiled=True,
    )
    query = prepare(queries)

    def shift(x, dim, step):
        stride = 8 if dim == "z" else 2
        table = []
        for i in range(32):
            at = (i // stride) % 4
            table.append((i, i + ((at + step) % 4 - at) * stride))
        return lax.ppermute(x, "pipe", table)

    axes = (("y", "z"), ("z", "y"))
    own = [both[:, half] for half in range(2)]
    after = [shift(own[half], axes[half][0], -1) for half in range(2)]
    before = [shift(own[half], axes[half][0], 1) for half in range(2)]
    opposite = [
        jnp.concatenate(
            [
                shift(before[half][: GROUP // 2], axes[half][0], 1),
                shift(after[half][GROUP // 2 :], axes[half][0], -1),
            ]
        )
        for half in range(2)
    ]
    before, query = lax.optimization_barrier((before, query))
    held = [
        jnp.stack([own[half], before[half], after[half], opposite[half]])
        for half in range(2)
    ]
    right = [shift(held[half], axes[half][1], 1) for half in range(2)]
    left = [shift(held[half], axes[half][1], -1) for half in range(2)]

    listed = [(0, 0), (0, -1), (0, 1), (0, 2)]
    places = (
        listed,
        [(f, n) for f in (-1, 1) for _, n in listed],
        [(2, n) for _, n in listed],
    )
    places = [([(f, n) for f, n in p], [(n, f) for f, n in p]) for p in places]

    def run(at, blocks, before):
        earlier = [sum((p[half] for p in places[:at]), []) for half in range(2)]
        return attend(
            slice_index, query, blocks, places[at], earlier, before, length, at == 2
        )

    state = run(0, [(held[half],) for half in range(2)], None)
    right, state = lax.optimization_barrier((right, state))
    far = [(shift(right[half], axes[half][1], 1),) for half in range(2)]
    state = run(1, list(zip(right, left)), state)
    return run(2, far, state)


def solution(mesh):
    return jax.shard_map(
        on_device,
        mesh=mesh,
        in_specs=(
            P(None, "pipe", "head"),
            P(("pipe", "head"), None),
            P(("pipe", "head"), None),
            P(),
        ),
        out_specs=P(None, "pipe", "head"),
        check_vma=False,
    )
```
